256 devices in a mesh: row: 8 (over z), col: 16 (over y, x), aux: 2 (over core).
Axes of the slice: x: 4, y: 4, z: 8, core: 2. Of those that a mesh axis runs over, the one named last changes fastest.
Arguments:
- panels: bfloat16 [64, 43200], P(('aux', 'row'), 'col'), may hold values from -6 to 6
- amplitudes: bfloat16 [10800, 43200], P('row', 'col'), may hold values from -0.03125 to 0.03125
- virt_coeff: bfloat16 [1500, 1350], replicated, may hold values from -0.15625 to 0.15625
- row_owner: int32 [1500, 1], replicated, may hold values from 0 to 127; in each aligned block of 1500 rows (0 to 1499, 1500 to 2999, ...) at most 24 rows name the same one
Outputs:
- delivered: bfloat16 [3072, 512], P(('row', 'col'), 'aux')
The draws below stay inside these ranges and needn't reach their ends.
Inputs may be any that keep to these rules, and one draw needn't show every extreme that they name: `row_owner`: no owner is named by more than 24 AO functions, a bound that some block reaches.
All inputs are finite; a program needn't handle non-finite values.
Results may differ from the reference program's by a relative error of at most 0.0017.
Values may be sent and summed in bfloat16 or wider, within the bound.
A program may use at most 64 MiB of HBM per device.

```python
import math
import jax
import jax.numpy as jnp
import numpy as np
from jax import lax

V = 1350
NAO = 1500
QCH = 64
I_SLAB = 8
J_BLK = 32
CAP = 24
N_ROW = 8
N_COL = 16


def block_levels(own_key, extent, cuts, smallest, high):
    def one(axis_at, blocks):
        draws = jax.random.uniform(jax.random.fold_in(jax.random.fold_in(own_key, 6), axis_at), (blocks,), jnp.float32, smallest / len(cuts), high / len(cuts))
        return jnp.repeat(jnp.exp(draws), extent[axis_at] // blocks).reshape((-1,) + (1,) * (len(extent) - axis_at - 1))

    gain = one(*cuts[0])
    for cut in cuts[1:]:
        gain = gain * one(*cut)
    return gain


def shared_out(stream_key, own, number, rows, amount, top, bound, lean):
    order = jax.random.permutation(stream_key, amount)
    packed, ordinary = shares(amount, rows * top, bound, lean, True), shares(amount, rows * top, bound, lean, False)
    places = jnp.arange(amount)

    def named(tallies, offset_by):
        used = int((tallies > 0).sum())
        fixed = max(1, used // 4)
        passed = fixed + (places - fixed + offset_by * (used - fixed)) % max(1, amount - fixed)
        return jnp.zeros((amount,), jnp.int32).at[order[jnp.where(places < fixed, places, passed)]].set(jnp.asarray(tallies, jnp.int32))

    tallies = jnp.where(number % 4 == 0, named(packed, number // 4), named(ordinary, number - number // 4 - 1))
    mixed = jax.random.permutation(jax.random.fold_in(own, 3), amount)
    source_of, sink = mixed[0:amount // 2 * 2:2], mixed[1:amount // 2 * 2:2]
    margin = jnp.minimum(tallies[source_of] - 1, bound - tallies[sink]) // 2
    margin = jnp.where((source_of == order[0]) | (sink == order[0]) | (tallies[sink] == 0), 0, jnp.maximum(margin, 0))
    passed = jax.random.randint(jax.random.fold_in(own, 4), (amount // 2,), 0, 1 << 20) % (margin + 1)
    tallies = tallies.at[source_of].add(-passed).at[sink].add(passed)
    members = jnp.searchsorted(jnp.cumsum(tallies), jnp.arange(rows * top), side="right").astype(jnp.int32)
    listing = members.reshape(top, rows).T
    listing = listing[jax.random.permutation(jax.random.fold_in(own, 1), rows)]
    offset_by = jax.random.randint(jax.random.fold_in(own, 2), (rows, 1), 0, top)
    return jnp.take_along_axis(listing, (jnp.arange(top)[None, :] + offset_by) % top, axis=1)


def shares(amount, total, reach, skew, full):
    portions = [(1 << 20) // math.isqrt(grade ** skew) + 1 for grade in range(1, amount + 1)]
    largest = reach if full else min(reach, max(-(-total // amount), total * portions[0] // sum(portions)))
    least = 1 if total - largest >= amount - 1 else 0
    holding, rest = [largest] + [least] * (amount - 1), total - largest - least * (amount - 1)
    while rest > 0:
        candidates = [i for i in range(1, amount) if holding[i] < largest] or [i for i in range(1, amount) if holding[i] < reach]
        pool, budget = sum([portions[i] for i in candidates]), rest
        for i in candidates:
            more = min(reach - holding[i], max(1, budget * portions[i] // pool), rest)
            holding[i] = holding[i] + more
            rest = rest - more
    return np.array(holding)


def normal_values(stream_key, dims, deviation, limit, shards=(), kind=jnp.bfloat16):
    entries = deviation * jax.random.normal(stream_key, dims, jnp.float32)
    if shards:
        entries = entries * block_levels(stream_key, dims, shards, -0.22, 0.18)
    return jnp.clip(entries, -limit, limit).astype(kind)


def setup_inputs(seed: int = 0) -> dict:
    seeds = jax.random.split(jax.random.key(seed), 5)
    panels = normal_values(seeds[0], (QCH, J_BLK * V), 1.0, 6.0, ((0, 16), (1, 16)))
    amplitudes = normal_values(seeds[1], (I_SLAB * V, J_BLK * V), (J_BLK * V) ** -0.5, 0.03125, ((0, 8), (1, 16)))
    virt_coeff = normal_values(seeds[2], (NAO, V), V ** -0.5, 0.15625)
    row_owner_keys = jax.random.split(jax.random.fold_in(seeds[3], 1), NAO // NAO)
    row_owner_turns = jax.random.permutation(jax.random.fold_in(seeds[3], 3), NAO // NAO)
    row_owner = jax.vmap(lambda own, number: shared_out(jax.random.fold_in(seeds[3], 2), own, number, NAO, N_ROW * N_COL, 1, CAP, 2))(row_owner_keys, row_owner_turns).reshape((NAO, 1))
    return {"panels": panels, "amplitudes": amplitudes, "virt_coeff": virt_coeff, "row_owner": row_owner}


def reference(panels, amplitudes, virt_coeff, row_owner):
    gamma = lax.dot_general(panels, amplitudes, (((1,), (1,)), ((), ())), preferred_element_type=jnp.float32)
    flat_gamma = gamma.reshape(QCH * I_SLAB, V)
    half = jnp.dot(flat_gamma, virt_coeff.astype(jnp.float32).T, precision=lax.Precision.HIGHEST)
    half = half.astype(jnp.bfloat16).reshape(QCH * I_SLAB, NAO)
    owners = row_owner[:, 0].astype(jnp.int32)
    count = N_ROW * N_COL
    onehot = (owners[:, None] == jnp.arange(count, dtype=jnp.int32)[None, :]).astype(jnp.int32)
    running = jnp.cumsum(onehot, axis=0).astype(jnp.int32) - 1
    slot = jnp.sum(running * onehot, axis=1).astype(jnp.int32)
    target = owners * CAP + slot
    delivered = jnp.zeros((count * CAP, QCH * I_SLAB), jnp.bfloat16)
    return delivered.at[target].set(half.T)
```

```python
import functools
import jax
import jax.numpy as jnp
from jax import lax
from jax.experimental import pallas as pl
from jax.experimental.pallas import tpu as pltpu
from jax.sharding import PartitionSpec as P

F32 = jnp.float32
BF16 = jnp.bfloat16
MESH = pl.DeviceIdType.MESH
NT = (((1,), (1,)), ((), ()))

LANES = 128
GROUPS = 4
CHUNK = 24
SIX = 6
EIGHT = 8


def split(x):
    hi = x.astype(BF16)
    lo = (x - hi.astype(F32)).astype(BF16)
    return hi, lo


def iota(shape, dim):
    return lax.broadcasted_iota(jnp.int32, shape, dim)


def kernel(
    rows_n,
    cols_n,
    panels,
    owner,
    amp,
    coeff_t,
    out,
    t_buf,
    w_buf,
    x_stage,
    x_all,
    g_t,
    own_pad,
    code,
    sel,
    expand,
    d_buf,
    r_buf,
    s_all,
    z_buf,
    z_all,
    o_buf,
    local_sem,
    xs,
    xr,
    ds,
    dr,
    ss,
    sr,
    zs,
    zr,
):
    me_r = lax.axis_index("row")
    me_c = lax.axis_index("col")
    q_own, depth = panels.shape
    virt, nao = coeff_t.shape
    q_dev = rows_n * q_own
    block = x_stage.shape[1]
    stride = CHUNK * cols_n

    cp_w = pltpu.make_async_copy(coeff_t, w_buf, local_sem.at[0])
    cp_t = pltpu.make_async_copy(amp, t_buf, local_sem.at[1])
    cp_w.start()
    cp_t.start()

    barrier = pltpu.get_barrier_semaphore()

    @pl.loop(1, rows_n)
    def _(k):
        pl.semaphore_signal(
            barrier, inc=1, device_id={"row": lax.rem(me_r + k, rows_n)}, device_id_type=MESH
        )

    @pl.loop(1, cols_n)
    def _(k):
        pl.semaphore_signal(
            barrier, inc=1, device_id={"col": lax.rem(me_c + k, cols_n)}, device_id_type=MESH
        )

    x_stage[...] = jnp.zeros_like(x_stage)
    for kb in range(GROUPS):
        width = min(block, depth - kb * block)
        x_stage[pl.ds(kb * q_own, q_own), pl.ds(0, width)] = panels[
            :, pl.ds(kb * block, width)
        ].astype(F32)
    tall = GROUPS * q_own
    x_all[pl.ds(pl.multiple_of(me_r * tall, tall), tall), :] = x_stage[...].astype(BF16)

    pl.semaphore_wait(barrier, rows_n - 1 + cols_n - 1)

    def panel_copy(owner_r, to):
        rows = x_all.at[pl.ds(pl.multiple_of(owner_r * tall, tall), tall), :]
        return pltpu.make_async_remote_copy(
            src_ref=rows,
            dst_ref=rows,
            send_sem=xs.at[to],
            recv_sem=xr.at[owner_r],
            device_id={"row": to},
            device_id_type=MESH,
        )

    @pl.loop(1, rows_n)
    def _(k):
        panel_copy(me_r, lax.rem(me_r + k, rows_n)).start()

    own_pad[...] = jnp.full_like(own_pad, -1)
    own_pad[:, pl.ds(0, nao)] = owner[...]
    count = rows_n * cols_n
    tri = (iota((256, 256), 0) < iota((256, 256), 1)).astype(BF16)
    carry = jnp.zeros((count, 1), F32)
    for b in range(own_pad.shape[1] // 256):
        names = own_pad[:, pl.ds(b * 256, 256)]
        hot = names == iota((count, 256), 0)
        ones = jnp.where(hot, 1.0, 0.0).astype(F32)
        before = jnp.dot(ones.astype(BF16), tri, preferred_element_type=F32) + carry
        slot = jnp.sum(ones * before, axis=0, keepdims=True)
        carry = carry + jnp.sum(ones, axis=1, keepdims=True)
        group = (
            jnp.where(slot >= SIX, 1.0, 0.0)
            + jnp.where(slot >= 2 * SIX, 1.0, 0.0)
            + jnp.where(slot >= 3 * SIX, 1.0, 0.0)
        )
        at_row = lax.div(names, jnp.int32(cols_n))
        at_col = names - at_row * cols_n
        place = group * (rows_n * EIGHT - SIX) + slot + at_row.astype(F32) * EIGHT
        code[:, pl.ds(b * 256, 256)] = jnp.where(at_col == me_c, place, -1.0)
    wide = GROUPS * rows_n * EIGHT
    perm = jnp.where(code[:, pl.ds(0, nao)] == iota((wide, nao), 0).astype(F32), 1.0, 0.0).astype(BF16)
    sel[...] = jnp.zeros_like(sel)
    cp_w.wait()
    sel[:, pl.ds(0, virt)] = lax.dot_general(
        perm, w_buf[...], NT, preferred_element_type=F32
    ).astype(BF16)

    for i in range(rows_n):
        a = iota((LANES, q_dev * rows_n), 0)
        n = iota((LANES, q_dev * rows_n), 1)
        spread = jnp.where(lax.rem(a, q_dev) * rows_n + i == n, 1.0, 0.0)
        expand[pl.ds(i * LANES, LANES), :] = spread.astype(BF16)

    @pl.loop(1, rows_n)
    def _(k):
        panel_copy(lax.rem(me_r + k, rows_n), me_r).wait_recv()

    for kb in range(GROUPS):
        n = iota((LANES, LANES), 0)
        m = iota((LANES, LANES), 1)
        q = lax.rem(n, q_dev)
        source = lax.div(q, q_own) * tall + kb * q_own + lax.rem(q, q_own)
        pick = jnp.where(source == m, 1.0, 0.0).astype(BF16)
        g = jnp.dot(pick, x_all[...], preferred_element_type=F32)
        g_t[pl.ds(kb * block, block), :] = g.T.astype(BF16)

    def lane_group(shape):
        return lax.div(iota(shape, 1), q_dev)

    def partial_copy(source, to):
        return pltpu.make_async_remote_copy(
            src_ref=d_buf.at[pl.ds(pl.multiple_of(to * CHUNK, CHUNK), CHUNK), :],
            dst_ref=r_buf.at[pl.ds(pl.multiple_of(source * CHUNK, CHUNK), CHUNK), :],
            send_sem=ds.at[to],
            recv_sem=dr.at[source],
            device_id={"col": to},
            device_id_type=MESH,
        )

    cp_t.wait()
    steps = 4
    part = stride // steps
    for step in range(steps):
        pieces, sizes = [], []
        for g in range(GROUPS):
            start = g * stride + step * part
            size = max(0, min(part, virt - start))
            if size:
                pieces.append(t_buf[pl.ds(start, size), :])
            sizes.append(size)
        dense = jnp.zeros((part, LANES), F32)
        groups = lane_group((part, LANES))
        for g in range(GROUPS):
            if sizes[g]:
                value = jnp.dot(pieces[g], g_t[pl.ds(0, depth), :], preferred_element_type=F32)
                if sizes[g] < part:
                    d_buf[pl.ds(step * part, part), :] = jnp.zeros((part, LANES), F32)
                    d_buf[pl.ds(step * part, sizes[g]), :] = value
                    value = d_buf[pl.ds(step * part, part), :]
                dense = jnp.where(groups == g, value, dense)
        d_buf[pl.ds(step * part, part), :] = dense
        per = cols_n // steps
        for j in range(per):
            to = step * per + j

            @pl.when(to != me_c)
            def _():
                partial_copy(me_c, to).start()

    def mine(ref):
        return ref[pl.ds(pl.multiple_of(me_c * CHUNK, CHUNK), CHUNK), :]

    total = mine(d_buf)
    for k in range(1, cols_n):
        source = lax.rem(me_c + k, cols_n)
        partial_copy(source, me_c).wait_recv()
        total = total + r_buf[pl.ds(pl.multiple_of(source * CHUNK, CHUNK), CHUNK), :]
    s_all[pl.ds(pl.multiple_of(me_c * CHUNK, CHUNK), CHUNK), :] = total

    def sum_copy(source, to):
        rows = s_all.at[pl.ds(pl.multiple_of(source * CHUNK, CHUNK), CHUNK), :]
        return pltpu.make_async_remote_copy(
            src_ref=rows,
            dst_ref=rows,
            send_sem=ss.at[to],
            recv_sem=sr.at[source],
            device_id={"col": to},
            device_id_type=MESH,
        )

    @pl.loop(1, cols_n)
    def _(k):
        sum_copy(me_c, lax.rem(me_c + k, cols_n)).start()

    @pl.loop(1, cols_n)
    def _(k):
        sum_copy(lax.rem(me_c + k, cols_n), me_c).wait_recv()

    hi, lo = split(s_all[...])
    both = jnp.concatenate([hi, lo], axis=1)
    y = jnp.zeros((wide, LANES), F32)
    groups = lane_group((wide, LANES))
    for g in range(GROUPS):
        x = jnp.dot(sel[:, pl.ds(g * stride, stride)], both, preferred_element_type=F32)
        y = y + jnp.where(groups == g, x[:, :LANES] + x[:, LANES:], 0.0)
    y = y + pltpu.roll(y, 2 * q_dev, 1)
    y = y + pltpu.roll(y, q_dev, 1)
    tall_z = rows_n * EIGHT
    z = jnp.zeros((tall_z, LANES), F32)
    groups = lane_group((tall_z, LANES))
    for g in range(GROUPS):
        z = jnp.where(groups == g, y[g * tall_z : (g + 1) * tall_z, :], z)
    z_buf[...] = z

    def slot_copy(source, to):
        return pltpu.make_async_remote_copy(
            src_ref=z_buf.at[pl.ds(pl.multiple_of(to * EIGHT, EIGHT), EIGHT), :],
            dst_ref=z_all.at[pl.ds(pl.multiple_of(source * EIGHT, EIGHT), EIGHT), :],
            send_sem=zs.at[to],
            recv_sem=zr.at[source],
            device_id={"row": to},
            device_id_type=MESH,
        )

    @pl.loop(1, rows_n)
    def _(k):
        slot_copy(me_r, lax.rem(me_r + k, rows_n)).start()

    own_rows = pl.ds(pl.multiple_of(me_r * EIGHT, EIGHT), EIGHT)
    z_all[own_rows, :] = z_buf[own_rows, :]

    @pl.loop(1, rows_n)
    def _(k):
        slot_copy(lax.rem(me_r + k, rows_n), me_r).wait_recv()

    groups = lane_group((EIGHT, LANES))
    lefts = []
    for i in range(rows_n):
        got = z_all[pl.ds(i * EIGHT, EIGHT), :]
        left = [jnp.where(groups == g, got, 0.0) for g in range(GROUPS)]
        lefts.append(jnp.concatenate(left, axis=0))
    left = jnp.concatenate(lefts, axis=1).astype(BF16)
    result = jnp.dot(left, expand[...], preferred_element_type=F32)
    for g in range(GROUPS):
        o_buf[pl.ds(g * SIX, SIX), :] = result[g * EIGHT : g * EIGHT + SIX, :]
    out[...] = o_buf[...].astype(BF16)

    @pl.loop(1, rows_n)
    def _(k):
        to = lax.rem(me_r + k, rows_n)
        panel_copy(me_r, to).wait_send()
        slot_copy(me_r, to).wait_send()

    @pl.loop(1, cols_n)
    def _(k):
        to = lax.rem(me_c + k, cols_n)
        partial_copy(me_c, to).wait_send()
        sum_copy(me_c, to).wait_send()


def shards(panels, amplitudes, virt_coeff, row_owner):
    rows_n = lax.axis_size("row")
    cols_n = lax.axis_size("col")
    q_own, depth = panels.shape
    nao, virt = virt_coeff.shape
    q_dev = rows_n * q_own
    block = -(-depth // (GROUPS * LANES)) * LANES
    stride = CHUNK * cols_n
    wide = GROUPS * rows_n * EIGHT
    vmem = pltpu.VMEM
    dma = pltpu.SemaphoreType.DMA
    return pl.pallas_call(
        functools.partial(kernel, rows_n, cols_n),
        out_shape=jax.ShapeDtypeStruct((GROUPS * SIX, q_dev * rows_n), BF16),
        in_specs=[
            pl.BlockSpec(memory_space=pltpu.VMEM),
            pl.BlockSpec(memory_space=pltpu.VMEM),
            pl.BlockSpec(memory_space=pl.ANY),
            pl.BlockSpec(memory_space=pl.ANY),
        ],
        out_specs=pl.BlockSpec(memory_space=pltpu.VMEM),
        scratch_shapes=[
            vmem(amplitudes.shape, BF16),
            vmem((virt, nao), BF16),
            vmem((GROUPS * q_own, block), F32),
            vmem((LANES, block), BF16),
            vmem((GROUPS * block, LANES), BF16),
            vmem((1, -(-nao // 256) * 256), jnp.int32),
            vmem((1, -(-nao // 256) * 256), F32),
            vmem((wide, GROUPS * stride), BF16),
            vmem((rows_n * LANES, q_dev * rows_n), BF16),
            vmem((stride, LANES), F32),
            vmem((stride, LANES), F32),
            vmem((stride, LANES), F32),
            vmem((rows_n * EIGHT, LANES), F32),
            vmem((rows_n * EIGHT, LANES), F32),
            vmem((GROUPS * SIX, q_dev * rows_n), F32),
            dma((2,)),
            dma((rows_n,)),
            dma((rows_n,)),
            dma((cols_n,)),
            dma((cols_n,)),
            dma((cols_n,)),
            dma((cols_n,)),
            dma((rows_n,)),
            dma((rows_n,)),
        ],
        compiler_params=pltpu.CompilerParams(
            collective_id=0, has_side_effects=True, vmem_limit_bytes=56 * 1024 * 1024
        ),
        cost_estimate=pl.CostEstimate(
            flops=2 * virt * depth * LANES, bytes_accessed=amplitudes.size * 2, transcendentals=0
        ),
        name="density",
    )(panels, row_owner.reshape(1, nao), amplitudes, virt_coeff.T)


def solution(mesh):
    placed = (P(("aux", "row"), "col"), P("row", "col"), P(), P())
    return jax.shard_map(
        shards, mesh=mesh, in_specs=placed, out_specs=P(("row", "col"), "aux"), check_vma=False
    )
```

```python
import functools
import jax
import jax.numpy as jnp
from jax import lax
from jax.experimental import pallas as pl
from jax.experimental.pallas import tpu as pltpu
from jax.sharding import PartitionSpec as P

F32 = jnp.float32
BF16 = jnp.bfloat16
MESH = pl.DeviceIdType.MESH
NT = (((1,), (1,)), ((), ()))

LANES = 128
BLOCKS = 4
WIDTH = 256
HEAD = 16
TAIL = 8
QUAD = 4


def split(x):
    hi = x.astype(BF16)
    lo = (x - hi.astype(F32)).astype(BF16)
    return jnp.concatenate([hi, lo], axis=0)


def iota(shape, dim):
    return lax.broadcasted_iota(jnp.int32, shape, dim)


def kernel(
    rows_n,
    cols_n,
    panels,
    owner,
    amp,
    coeff_t,
    out,
    t_buf,
    w_buf,
    p_buf,
    o_buf,
    names,
    x_stage,
    x_all,
    place,
    spread,
    expand,
    d_buf,
    r_buf,
    z_buf,
    z_all,
    local_sem,
    xs,
    xr,
    ds,
    dr,
    zs,
    zr,
):
    me_r = lax.axis_index("row")
    me_c = lax.axis_index("col")
    q_own, depth = panels.shape
    virt, nao = coeff_t.shape
    q_dev = rows_n * q_own
    chunks = x_all.shape[0]
    block = chunks * WIDTH
    tall = BLOCKS * q_own
    count = rows_n * cols_n
    dense = q_dev + q_dev // 2
    pair = 3 * LANES

    barrier = pltpu.get_barrier_semaphore()
    for k in range(1, rows_n):
        pl.semaphore_signal(
            barrier, inc=1, device_id={"row": lax.rem(me_r + k, rows_n)}, device_id_type=MESH
        )
    for k in range(1, cols_n):
        pl.semaphore_signal(
            barrier, inc=1, device_id={"col": lax.rem(me_c + k, cols_n)}, device_id_type=MESH
        )
    cp_p = pltpu.make_async_copy(panels, p_buf, local_sem.at[0])
    cp_o = pltpu.make_async_copy(owner, o_buf, local_sem.at[1])
    cp_t = pltpu.make_async_copy(amp, t_buf, local_sem.at[2])
    cp_w = pltpu.make_async_copy(coeff_t, w_buf, local_sem.at[3])
    cp_p.start()
    cp_o.start()
    cp_t.start()
    cp_w.start()

    x_stage[...] = jnp.zeros_like(x_stage)
    cp_p.wait()
    for kb in range(BLOCKS):
        width = min(block, depth - kb * block)
        x_stage[pl.ds(kb * q_own, q_own), pl.ds(0, width)] = p_buf[
            :, pl.ds(kb * block, width)
        ].astype(F32)
    own_rows = pl.ds(pl.multiple_of(me_r * tall, tall), tall)
    for t in range(chunks):
        x_all[t, own_rows, :] = x_stage[:, pl.ds(t * WIDTH, WIDTH)].astype(BF16)

    pl.semaphore_wait(barrier, rows_n - 1 + cols_n - 1)

    def panel_copy(t, source, to):
        rows = x_all.at[t, pl.ds(pl.multiple_of(source * tall, tall), tall), :]
        return pltpu.make_async_remote_copy(
            src_ref=rows,
            dst_ref=rows,
            send_sem=xs.at[t, to],
            recv_sem=xr.at[t, source],
            device_id={"row": to},
            device_id_type=MESH,
        )

    for t in range(chunks):
        for k in (4, 3, 5, 2, 6, 1, 7):
            panel_copy(t, me_r, lax.rem(me_r + k, rows_n)).start()

    names[...] = jnp.full_like(names, -1)
    cp_o.wait()
    names[:, pl.ds(0, nao)] = o_buf[...]
    tri = (iota((WIDTH, WIDTH), 0) < iota((WIDTH, WIDTH), 1)).astype(BF16)
    carry = jnp.zeros((count, 1), F32)
    for b in range(names.shape[1] // WIDTH):
        name = names[:, pl.ds(b * WIDTH, WIDTH)]
        ones = jnp.where(name == iota((count, WIDTH), 0), 1.0, 0.0).astype(F32)
        before = jnp.dot(ones.astype(BF16), tri, preferred_element_type=F32) + carry
        slot = jnp.sum(ones * before, axis=0, keepdims=True)
        carry = carry + jnp.sum(ones, axis=1, keepdims=True)
        at_row = lax.div(name, jnp.int32(cols_n))
        at_col = name - at_row * cols_n
        at_pair = lax.div(at_col, jnp.int32(2))
        odd = at_col - at_pair * 2
        base = (at_pair * pair + at_row * HEAD).astype(F32)
        early = base + (odd * LANES).astype(F32) + slot
        late = base + (odd * TAIL + (2 * LANES - HEAD)).astype(F32) + slot
        lane = jnp.where(slot < HEAD, early, late)
        lane = jnp.where(name < 0, -1.0, lane)
        place[pl.ds(b * WIDTH, WIDTH), :] = jnp.broadcast_to(lane, (LANES, WIDTH)).T

    @pl.loop(0, spread.shape[1] // LANES)
    def _(b):
        at = (iota((nao, LANES), 1) + b * LANES).astype(F32)
        hot = jnp.where(place[pl.ds(0, nao), :] == at, 1.0, 0.0)
        spread[:, pl.ds(pl.multiple_of(b * LANES, LANES), LANES)] = hot.astype(BF16)

    for i in range(rows_n):
        a = iota((LANES, rows_n * q_dev), 0)
        n = iota((LANES, rows_n * q_dev), 1)
        head = jnp.where((a < q_dev) & (n == a * rows_n + i), 1.0, 0.0)
        tail = jnp.where(
            (a >= q_dev) & (a < dense) & (lax.rem(n, LANES) == (a - q_dev) * rows_n + i), 1.0, 0.0
        )
        expand[pl.ds(i * LANES, LANES), :] = jnp.concatenate([head, tail], axis=1).astype(BF16)

    cp_t.wait()
    partial = jnp.zeros((q_dev, virt), F32)
    for t in range(chunks):

        @pl.loop(1, rows_n)
        def _(k):
            panel_copy(t, lax.rem(me_r + k, rows_n), me_r).wait_recv()

        for kb in range(BLOCKS):
            start = kb * block + t * WIDTH
            width = min(WIDTH, depth - start)
            if width <= 0:
                continue
            q = iota((q_dev, LANES), 0)
            source = lax.div(q, q_own) * tall + kb * q_own + lax.rem(q, q_own)
            pick = jnp.where(source == iota((q_dev, LANES), 1), 1.0, 0.0).astype(BF16)
            g = jnp.dot(pick, x_all[t], preferred_element_type=F32).astype(BF16)
            partial = partial + lax.dot_general(
                g[:, :width], t_buf[:, pl.ds(start, width)], NT, preferred_element_type=F32
            )

    cp_w.wait()
    half = jnp.dot(split(partial), w_buf[...], preferred_element_type=F32)
    half = split(half[:q_dev] + half[q_dev:])

    def partial_copy(source, to):
        return pltpu.make_async_remote_copy(
            src_ref=d_buf.at[to],
            dst_ref=r_buf.at[source],
            send_sem=ds.at[to],
            recv_sem=dr.at[source],
            device_id={"col": to},
            device_id_type=MESH,
        )

    quads = cols_n // QUAD
    my_quad = lax.div(me_c, QUAD)
    lower = lax.rem(iota((q_dev // 2, LANES), 1), 2 * TAIL) < TAIL
    for step in range(quads):
        quad = lax.rem(my_quad + (2, 1, 3, 0)[step], quads)
        lanes = QUAD // 2 * pair
        part = spread[:, pl.ds(pl.multiple_of(quad * lanes, lanes), lanes)]
        slots = jnp.dot(half, part, preferred_element_type=F32)
        slots = slots[:q_dev] + slots[q_dev:]
        for j in range(QUAD):
            to = quad * QUAD + j
            first = j // 2 * pair
            head = slots[:, first + j % 2 * LANES : first + (j % 2 + 1) * LANES]
            tail = slots[:, first + 2 * LANES : first + 3 * LANES]
            upper_q, lower_q = tail[: q_dev // 2], tail[q_dev // 2 :]
            if j % 2:
                upper_q = pltpu.roll(upper_q, LANES - TAIL, 1)
            else:
                lower_q = pltpu.roll(lower_q, TAIL, 1)
            d_buf[to, pl.ds(0, q_dev), :] = head
            d_buf[to, pl.ds(q_dev, q_dev // 2), :] = jnp.where(lower, upper_q, lower_q)

            @pl.when(to != me_c)
            def _():
                partial_copy(me_c, to).start()

    total = d_buf[me_c]
    for k in range(1, cols_n):
        source = lax.rem(me_c + k, cols_n)
        partial_copy(source, me_c).wait_recv()
        total = total + r_buf[source]
    total = jnp.concatenate([total, jnp.zeros((LANES - dense, LANES), F32)], axis=0)
    z_buf[...] = total.T.astype(BF16)

    def slot_copy(source, to):
        return pltpu.make_async_remote_copy(
            src_ref=z_buf.at[pl.ds(pl.multiple_of(to * HEAD, HEAD), HEAD), :],
            dst_ref=z_all.at[pl.ds(pl.multiple_of(source * HEAD, HEAD), HEAD), :],
            send_sem=zs.at[to],
            recv_sem=zr.at[source],
            device_id={"row": to},
            device_id_type=MESH,
        )

    for k in (4, 3, 5, 2, 6, 1, 7):
        slot_copy(me_r, lax.rem(me_r + k, rows_n)).start()
    own = pl.ds(pl.multiple_of(me_r * HEAD, HEAD), HEAD)
    z_all[own, :] = z_buf[own, :]

    @pl.loop(1, rows_n)
    def _(k):
        slot_copy(lax.rem(me_r + k, rows_n), me_r).wait_recv()

    got = jnp.concatenate([z_all[pl.ds(i * HEAD, HEAD), :] for i in range(rows_n)], axis=1)
    result = jnp.dot(got, expand[...], preferred_element_type=F32)
    wide = rows_n * q_dev
    tail = jnp.concatenate(
        [result[:TAIL, wide : wide + LANES], result[TAIL:, wide + LANES :]], axis=1
    )
    out[...] = jnp.concatenate([result[:, :wide], tail], axis=0).astype(BF16)

    @pl.loop(1, rows_n)
    def _(k):
        to = lax.rem(me_r + k, rows_n)
        for t in range(chunks):
            panel_copy(t, me_r, to).wait_send()
        slot_copy(me_r, to).wait_send()

    @pl.loop(1, cols_n)
    def _(k):
        partial_copy(me_c, lax.rem(me_c + k, cols_n)).wait_send()


def shards(panels, amplitudes, virt_coeff, row_owner):
    rows_n = lax.axis_size("row")
    cols_n = lax.axis_size("col")
    q_own, depth = panels.shape
    nao, virt = virt_coeff.shape
    q_dev = rows_n * q_own
    chunks = -(-depth // (BLOCKS * WIDTH))
    tall = BLOCKS * q_own
    padded = -(-nao // WIDTH) * WIDTH
    dense = q_dev + q_dev // 2
    vmem = pltpu.VMEM
    dma = pltpu.SemaphoreType.DMA
    return pl.pallas_call(
        functools.partial(kernel, rows_n, cols_n),
        out_shape=jax.ShapeDtypeStruct((HEAD + TAIL, rows_n * q_dev), BF16),
        in_specs=[pl.BlockSpec(memory_space=pl.ANY)] * 4,
        out_specs=pl.BlockSpec(memory_space=pltpu.VMEM),
        scratch_shapes=[
            vmem(amplitudes.shape, BF16),
            vmem((virt, nao), BF16),
            vmem(panels.shape, BF16),
            vmem((1, nao), jnp.int32),
            vmem((1, padded), jnp.int32),
            vmem((tall, chunks * WIDTH), F32),
            vmem((chunks, rows_n * tall, WIDTH), BF16),
            vmem((padded, LANES), F32),
            vmem((nao, cols_n // 2 * 3 * LANES), BF16),
            vmem((rows_n * LANES, 2 * rows_n * q_dev), BF16),
            vmem((cols_n, dense, LANES), F32),
            vmem((cols_n, dense, LANES), F32),
            vmem((rows_n * HEAD, LANES), BF16),
            vmem((rows_n * HEAD, LANES), BF16),
            dma((4,)),
            dma((chunks, rows_n)),
            dma((chunks, rows_n)),
            dma((cols_n,)),
            dma((cols_n,)),
            dma((rows_n,)),
            dma((rows_n,)),
        ],
        compiler_params=pltpu.CompilerParams(
            collective_id=0, has_side_effects=True, vmem_limit_bytes=56 * 1024 * 1024
        ),
        cost_estimate=pl.CostEstimate(
            flops=2 * virt * depth * LANES, bytes_accessed=amplitudes.size * 2, transcendentals=0
        ),
        name="density",
    )(panels, row_owner.reshape(1, nao), amplitudes, virt_coeff.T)


def solution(mesh):
    placed = (P(("aux", "row"), "col"), P("row", "col"), P(), P())
    return jax.shard_map(
        shards, mesh=mesh, in_specs=placed, out_specs=P(("row", "col"), "aux"), check_vma=False
    )
```

```python
import functools
import jax
import jax.numpy as jnp
from jax import lax
from jax.experimental import pallas as pl
from jax.experimental.pallas import tpu as pltpu
from jax.sharding import PartitionSpec as P

F32 = jnp.float32
BF16 = jnp.bfloat16
MESH = pl.DeviceIdType.MESH
NT = (((1,), (1,)), ((), ()))

LANES = 128
BLOCKS = 4
WIDTH = 256
HEAD = 16
TAIL = 8
QUAD = 4


def split(x):
    hi = x.astype(BF16)
    lo = (x - hi.astype(F32)).astype(BF16)
    return jnp.concatenate([hi, lo], axis=0)


def iota(shape, dim):
    return lax.broadcasted_iota(jnp.int32, shape, dim)


def kernel(
    rows_n,
    cols_n,
    aux_n,
    panels,
    owner,
    amp,
    coeff_t,
    out,
    t_buf,
    w_buf,
    p_buf,
    o_buf,
    names,
    x_stage,
    x_all,
    place,
    spread,
    expand,
    d_buf,
    r_buf,
    z_buf,
    z_all,
    local_sem,
    xs,
    xr,
    ds,
    dr,
    zs,
    zr,
):
    me_r = lax.axis_index("row")
    me_c = lax.axis_index("col")
    me_a = lax.axis_index("aux")
    worker = me_a == aux_n - 1
    q_own, depth = panels.shape
    virt, nao = coeff_t.shape
    q_dev = rows_n * q_own
    q_all = aux_n * q_dev
    chunks = x_all.shape[0]
    block = chunks * WIDTH
    tall = BLOCKS * q_own
    count = rows_n * cols_n
    sources = aux_n * rows_n
    dense = q_dev + q_dev // 2
    pair = 3 * LANES
    order = (4, 3, 5, 2, 6, 1, 7)

    def row_at(k):
        return lax.rem(me_r + k, rows_n)

    barrier = pltpu.get_barrier_semaphore()

    def greet(**to):
        pl.semaphore_signal(barrier, inc=1, device_id=to, device_id_type=MESH)

    for k in order:
        greet(row=row_at(k), aux=aux_n - 1)

    cp_p = pltpu.make_async_copy(panels, p_buf, local_sem.at[0])
    cp_o = pltpu.make_async_copy(owner, o_buf, local_sem.at[1])
    cp_t = pltpu.make_async_copy(amp, t_buf, local_sem.at[2])
    cp_w = pltpu.make_async_copy(coeff_t, w_buf, local_sem.at[3])
    cp_p.start()

    @pl.when(worker)
    def _():
        for k in order + (0,):
            greet(row=row_at(k), aux=0)
        cp_o.start()
        cp_t.start()
        cp_w.start()
        for k in range(1, cols_n):
            greet(col=lax.rem(me_c + k, cols_n))

    @pl.when(jnp.logical_not(worker))
    def _():
        greet(aux=aux_n - 1)

    x_stage[...] = jnp.zeros_like(x_stage)
    cp_p.wait()
    for t in range(chunks):
        for kb in range(BLOCKS):
            start = (t * BLOCKS + kb) * WIDTH
            width = min(WIDTH, depth - start)
            if width > 0:
                x_stage[t, pl.ds(kb * q_own, q_own), pl.ds(0, width)] = p_buf[
                    :, pl.ds(start, width)
                ].astype(F32)
    me_source = me_a * rows_n + me_r
    for t in range(chunks):
        x_all[t, pl.ds(pl.multiple_of(me_source * tall, tall), tall), :] = x_stage[t].astype(BF16)

    def panel_copy(t, source, to):
        rows = x_all.at[t, pl.ds(pl.multiple_of(source * tall, tall), tall), :]
        return pltpu.make_async_remote_copy(
            src_ref=rows,
            dst_ref=rows,
            send_sem=xs.at[t, to],
            recv_sem=xr.at[t, source],
            device_id={"row": to, "aux": aux_n - 1},
            device_id_type=MESH,
        )

    def partial_copy(source, to):
        return pltpu.make_async_remote_copy(
            src_ref=d_buf.at[to],
            dst_ref=r_buf.at[source],
            send_sem=ds.at[to],
            recv_sem=dr.at[source],
            device_id={"col": to},
            device_id_type=MESH,
        )

    def slot_copy(source, to, aux):
        return pltpu.make_async_remote_copy(
            src_ref=z_buf.at[aux, pl.ds(pl.multiple_of(to * HEAD, HEAD), HEAD), :],
            dst_ref=z_all.at[pl.ds(pl.multiple_of(source * HEAD, HEAD), HEAD), :],
            send_sem=zs.at[aux, to],
            recv_sem=zr.at[source],
            device_id={"row": to, "aux": aux},
            device_id_type=MESH,
        )

    @pl.when(worker)
    def _():
        pl.semaphore_wait(barrier, sources - 1 + cols_n - 1)

    @pl.when(jnp.logical_not(worker))
    def _():
        pl.semaphore_wait(barrier, rows_n)

    for t in range(chunks):
        for k in order:
            panel_copy(t, me_source, row_at(k)).start()

        @pl.when(jnp.logical_not(worker))
        def _():
            panel_copy(t, me_source, me_r).start()

    for i in range(rows_n):
        a = iota((LANES, rows_n * q_dev), 0)
        n = iota((LANES, rows_n * q_dev), 1)
        head = jnp.where((a < q_dev) & (n == a * rows_n + i), 1.0, 0.0)
        tail = jnp.where(
            (a >= q_dev) & (a < dense) & (lax.rem(n, LANES) == (a - q_dev) * rows_n + i), 1.0, 0.0
        )
        expand[pl.ds(i * LANES, LANES), :] = jnp.concatenate([head, tail], axis=1).astype(BF16)

    @pl.when(worker)
    def _():
        names[...] = jnp.full_like(names, -1)
        cp_o.wait()
        names[:, pl.ds(0, nao)] = o_buf[...]
        tri = (iota((WIDTH, WIDTH), 0) < iota((WIDTH, WIDTH), 1)).astype(BF16)
        carry = jnp.zeros((count, 1), F32)
        for b in range(names.shape[1] // WIDTH):
            name = names[:, pl.ds(b * WIDTH, WIDTH)]
            ones = jnp.where(name == iota((count, WIDTH), 0), 1.0, 0.0).astype(F32)
            before = jnp.dot(ones.astype(BF16), tri, preferred_element_type=F32) + carry
            slot = jnp.sum(ones * before, axis=0, keepdims=True)
            carry = carry + jnp.sum(ones, axis=1, keepdims=True)
            at_row = lax.div(name, jnp.int32(cols_n))
            at_col = name - at_row * cols_n
            at_pair = lax.div(at_col, jnp.int32(2))
            odd = at_col - at_pair * 2
            base = (at_pair * pair + at_row * HEAD).astype(F32)
            early = base + (odd * LANES).astype(F32) + slot
            late = base + (odd * TAIL + (2 * LANES - HEAD)).astype(F32) + slot
            lane = jnp.where(slot < HEAD, early, late)
            lane = jnp.where(name < 0, -1.0, lane)
            place[pl.ds(b * WIDTH, WIDTH), :] = jnp.broadcast_to(lane, (LANES, WIDTH)).T

        @pl.loop(0, spread.shape[1] // LANES)
        def _(b):
            at = (iota((nao, LANES), 1) + b * LANES).astype(F32)
            hot = jnp.where(place[pl.ds(0, nao), :] == at, 1.0, 0.0)
            spread[:, pl.ds(pl.multiple_of(b * LANES, LANES), LANES)] = hot.astype(BF16)

        cp_t.wait()
        partial = jnp.zeros((q_all, virt), F32)
        for t in range(chunks):

            @pl.loop(1, sources)
            def _(k):
                panel_copy(t, lax.rem(me_source + k, sources), me_r).wait_recv()

            for kb in range(BLOCKS):
                start = (t * BLOCKS + kb) * WIDTH
                width = min(WIDTH, depth - start)
                if width <= 0:
                    continue
                wide = sources * tall
                q = iota((q_all, wide), 0)
                source = lax.div(q, q_own) * tall + kb * q_own + lax.rem(q, q_own)
                pick = jnp.where(source == iota((q_all, wide), 1), 1.0, 0.0).astype(BF16)
                g = jnp.dot(pick, x_all[t], preferred_element_type=F32).astype(BF16)
                partial = partial + lax.dot_general(
                    g[:, :width], t_buf[:, pl.ds(start, width)], NT, preferred_element_type=F32
                )

        cp_w.wait()
        half = jnp.dot(split(partial), w_buf[...], preferred_element_type=F32)
        half = split(half[:q_all] + half[q_all:])

        quads = cols_n // QUAD
        my_quad = lax.div(me_c, QUAD)
        lower = lax.rem(iota((q_dev // 2, LANES), 1), 2 * TAIL) < TAIL
        for step in range(quads):
            quad = lax.rem(my_quad + (2, 1, 3, 0)[step], quads)
            lanes = QUAD // 2 * pair
            part = spread[:, pl.ds(pl.multiple_of(quad * lanes, lanes), lanes)]
            slots = jnp.dot(half, part, preferred_element_type=F32)
            slots = slots[:q_all] + slots[q_all:]
            for j in range(QUAD):
                to = quad * QUAD + j
                first = j // 2 * pair
                for aux in range(aux_n):
                    rows = slots[aux * q_dev : (aux + 1) * q_dev]
                    head = rows[:, first + j % 2 * LANES : first + (j % 2 + 1) * LANES]
                    tail = rows[:, first + 2 * LANES : first + 3 * LANES]
                    upper_q, lower_q = tail[: q_dev // 2], tail[q_dev // 2 :]
                    if j % 2:
                        upper_q = pltpu.roll(upper_q, LANES - TAIL, 1)
                    else:
                        lower_q = pltpu.roll(lower_q, TAIL, 1)
                    d_buf[to, pl.ds(aux * dense, q_dev), :] = head
                    d_buf[to, pl.ds(aux * dense + q_dev, q_dev // 2), :] = jnp.where(
                        lower, upper_q, lower_q
                    )

                @pl.when(to != me_c)
                def _():
                    partial_copy(me_c, to).start()

        total = d_buf[me_c]
        for k in range(1, cols_n):
            source = lax.rem(me_c + k, cols_n)
            partial_copy(source, me_c).wait_recv()
            total = total + r_buf[source]
        for aux in range(aux_n):
            own = total[aux * dense : (aux + 1) * dense]
            own = jnp.concatenate([own, jnp.zeros((LANES - dense, LANES), F32)], axis=0)
            z_buf[aux] = own.T.astype(BF16)
            for k in order:
                slot_copy(me_r, row_at(k), aux).start()
            if aux < aux_n - 1:
                slot_copy(me_r, me_r, aux).start()
        own = pl.ds(pl.multiple_of(me_r * HEAD, HEAD), HEAD)
        z_all[own, :] = z_buf[aux_n - 1, own, :]

    @pl.loop(1, rows_n)
    def _(k):
        slot_copy(row_at(k), me_r, me_a).wait_recv()

    @pl.when(jnp.logical_not(worker))
    def _():
        slot_copy(me_r, me_r, me_a).wait_recv()

    got = jnp.concatenate([z_all[pl.ds(i * HEAD, HEAD), :] for i in range(rows_n)], axis=1)
    result = jnp.dot(got, expand[...], preferred_element_type=F32)
    wide = rows_n * q_dev
    tail = jnp.concatenate(
        [result[:TAIL, wide : wide + LANES], result[TAIL:, wide + LANES :]], axis=1
    )
    out[...] = jnp.concatenate([result[:, :wide], tail], axis=0)

    @pl.loop(1, rows_n)
    def _(k):
        for t in range(chunks):
            panel_copy(t, me_source, row_at(k)).wait_send()

    @pl.when(jnp.logical_not(worker))
    def _():
        for t in range(chunks):
            panel_copy(t, me_source, me_r).wait_send()

    @pl.when(worker)
    def _():
        @pl.loop(1, cols_n)
        def _(k):
            partial_copy(me_c, lax.rem(me_c + k, cols_n)).wait_send()

        for aux in range(aux_n):
            for k in order:
                slot_copy(me_r, row_at(k), aux).wait_send()
            if aux < aux_n - 1:
                slot_copy(me_r, me_r, aux).wait_send()


def shards(panels, amplitudes, virt_coeff, row_owner):
    rows_n = lax.axis_size("row")
    cols_n = lax.axis_size("col")
    aux_n = lax.axis_size("aux")
    q_own, depth = panels.shape
    nao, virt = virt_coeff.shape
    q_dev = rows_n * q_own
    chunks = -(-depth // (BLOCKS * WIDTH))
    tall = BLOCKS * q_own
    padded = -(-nao // WIDTH) * WIDTH
    dense = q_dev + q_dev // 2
    vmem = pltpu.VMEM
    dma = pltpu.SemaphoreType.DMA
    return pl.pallas_call(
        functools.partial(kernel, rows_n, cols_n, aux_n),
        out_shape=jax.ShapeDtypeStruct((HEAD + TAIL, rows_n * q_dev), F32),
        in_specs=[pl.BlockSpec(memory_space=pl.ANY)] * 4,
        out_specs=pl.BlockSpec(memory_space=pltpu.VMEM),
        scratch_shapes=[
            vmem(amplitudes.shape, BF16),
            vmem((virt, nao), BF16),
            vmem(panels.shape, BF16),
            vmem((1, nao), jnp.int32),
            vmem((1, padded), jnp.int32),
            vmem((chunks, tall, WIDTH), F32),
            vmem((chunks, aux_n * rows_n * tall, WIDTH), BF16),
            vmem((padded, LANES), F32),
            vmem((nao, cols_n // 2 * 3 * LANES), BF16),
            vmem((rows_n * LANES, 2 * rows_n * q_dev), BF16),
            vmem((cols_n, aux_n * dense, LANES), F32),
            vmem((cols_n, aux_n * dense, LANES), F32),
            vmem((aux_n, rows_n * HEAD, LANES), BF16),
            vmem((rows_n * HEAD, LANES), BF16),
            dma((4,)),
            dma((chunks, rows_n)),
            dma((chunks, aux_n * rows_n)),
            dma((cols_n,)),
            dma((cols_n,)),
            dma((aux_n, rows_n)),
            dma((rows_n,)),
        ],
        compiler_params=pltpu.CompilerParams(
            collective_id=0, has_side_effects=True, vmem_limit_bytes=56 * 1024 * 1024
        ),
        cost_estimate=pl.CostEstimate(
            flops=2 * virt * depth * LANES, bytes_accessed=amplitudes.size * 2, transcendentals=0
        ),
        name="density",
    )(panels, row_owner.reshape(1, nao), amplitudes, virt_coeff.T).astype(BF16)


def solution(mesh):
    placed = (P(("aux", "row"), "col"), P("row", "col"), P(), P())
    return jax.shard_map(
        shards, mesh=mesh, in_specs=placed, out_specs=P(("row", "col"), "aux"), check_vma=False
    )
```

```python
import functools
import jax
import jax.numpy as jnp
from jax import lax
from jax.experimental import pallas as pl
from jax.experimental.pallas import tpu as pltpu
from jax.sharding import PartitionSpec as P

F32 = jnp.float32
BF16 = jnp.bfloat16
MESH = pl.DeviceIdType.MESH
NT = (((1,), (1,)), ((), ()))

LANES = 128
BLOCKS = 4
WIDTH = 256
HEAD = 16
TAIL = 8
QUAD = 4


def split(x):
    hi = x.astype(BF16)
    lo = (x - hi.astype(F32)).astype(BF16)
    return jnp.concatenate([hi, lo], axis=0)


def iota(shape, dim):
    return lax.broadcasted_iota(jnp.int32, shape, dim)


def kernel(
    rows_n,
    cols_n,
    panels,
    owner,
    amp,
    coeff_t,
    out,
    t_buf,
    w_buf,
    p_buf,
    o_buf,
    names,
    x_stage,
    x_all,
    place,
    spread,
    expand,
    d_buf,
    r_buf,
    z_buf,
    z_all,
    local_sem,
    xs,
    xr,
    ds,
    dr,
    zs,
    zr,
):
    me_r = lax.axis_index("row")
    me_c = lax.axis_index("col")
    me_a = lax.axis_index("aux")
    q_own, depth = panels.shape
    virt, nao = coeff_t.shape
    q_dev = rows_n * q_own
    chunks = x_all.shape[0]
    tall = BLOCKS * q_own
    count = rows_n * cols_n
    dense = q_dev + q_dev // 2
    pair = 3 * LANES
    order = (4, 3, 5, 2, 6, 1, 7)
    far = (10, 6, 9, 11, 5, 7, 8, 2, 14, 13, 15, 12, 4, 3, 1)

    def row_at(k):
        return lax.rem(me_r + k, rows_n)

    barrier = pltpu.get_barrier_semaphore()
    def greet(**to):
        pl.semaphore_signal(barrier, inc=1, device_id=to, device_id_type=MESH)

    for k in order:
        greet(row=row_at(k))
    for k in order + (0,):
        greet(row=row_at(k), aux=1 - me_a)
    for k in far:
        greet(col=lax.rem(me_c + k, cols_n), aux=1 - me_a)
    cp_p = pltpu.make_async_copy(panels, p_buf, local_sem.at[0])
    cp_o = pltpu.make_async_copy(owner, o_buf, local_sem.at[1])
    cp_t = pltpu.make_async_copy(amp, t_buf, local_sem.at[2])
    cp_w = pltpu.make_async_copy(coeff_t, w_buf, local_sem.at[3])
    cp_p.start()
    cp_o.start()
    cp_t.start()
    cp_w.start()

    x_stage[...] = jnp.zeros_like(x_stage)
    cp_p.wait()
    for t in range(chunks):
        for kb in range(BLOCKS):
            start = (t * BLOCKS + kb) * WIDTH
            width = min(WIDTH, depth - start)
            if width > 0:
                x_stage[t, pl.ds(kb * q_own, q_own), pl.ds(0, width)] = p_buf[
                    :, pl.ds(start, width)
                ].astype(F32)
    own_rows = pl.ds(pl.multiple_of(me_r * tall, tall), tall)
    for t in range(chunks):
        x_all[t, own_rows, :] = x_stage[t].astype(BF16)

    pl.semaphore_wait(barrier, 2 * (rows_n - 1) + cols_n)

    def panel_copy(t, source, to):
        rows = x_all.at[t, pl.ds(pl.multiple_of(source * tall, tall), tall), :]
        return pltpu.make_async_remote_copy(
            src_ref=rows,
            dst_ref=rows,
            send_sem=xs.at[t, to],
            recv_sem=xr.at[t, source],
            device_id={"row": to},
            device_id_type=MESH,
        )

    for t in range(chunks):
        for k in order:
            panel_copy(t, me_r, row_at(k)).start()

    names[...] = jnp.full_like(names, -1)
    cp_o.wait()
    names[:, pl.ds(0, nao)] = o_buf[...]
    tri = (iota((WIDTH, WIDTH), 0) < iota((WIDTH, WIDTH), 1)).astype(BF16)
    carry = jnp.zeros((count, 1), F32)
    for b in range(names.shape[1] // WIDTH):
        name = names[:, pl.ds(b * WIDTH, WIDTH)]
        ones = jnp.where(name == iota((count, WIDTH), 0), 1.0, 0.0).astype(F32)
        before = jnp.dot(ones.astype(BF16), tri, preferred_element_type=F32) + carry
        slot = jnp.sum(ones * before, axis=0, keepdims=True)
        carry = carry + jnp.sum(ones, axis=1, keepdims=True)
        at_row = lax.div(name, jnp.int32(cols_n))
        at_col = name - at_row * cols_n
        at_pair = lax.div(at_col, jnp.int32(2))
        odd = at_col - at_pair * 2
        base = (at_pair * pair + at_row * HEAD).astype(F32)
        early = base + (odd * LANES).astype(F32) + slot
        late = base + (odd * TAIL + (2 * LANES - HEAD)).astype(F32) + slot
        lane = jnp.where(slot < HEAD, early, late)
        lane = jnp.where(name < 0, -1.0, lane)
        place[pl.ds(b * WIDTH, WIDTH), :] = jnp.broadcast_to(lane, (LANES, WIDTH)).T

    @pl.loop(0, spread.shape[1] // LANES)
    def _(b):
        at = (iota((nao, LANES), 1) + b * LANES).astype(F32)
        hot = jnp.where(place[pl.ds(0, nao), :] == at, 1.0, 0.0)
        spread[:, pl.ds(pl.multiple_of(b * LANES, LANES), LANES)] = hot.astype(BF16)

    for i in range(rows_n):
        a = iota((LANES, rows_n * q_dev), 0)
        n = iota((LANES, rows_n * q_dev), 1)
        head = jnp.where((a < q_dev) & (n == a * rows_n + i), 1.0, 0.0)
        tail = jnp.where(
            (a >= q_dev) & (a < dense) & (lax.rem(n, LANES) == (a - q_dev) * rows_n + i), 1.0, 0.0
        )
        expand[pl.ds(i * LANES, LANES), :] = jnp.concatenate([head, tail], axis=1).astype(BF16)

    cp_t.wait()
    partial = jnp.zeros((q_dev, virt), F32)
    for t in range(chunks):

        @pl.loop(1, rows_n)
        def _(k):
            panel_copy(t, lax.rem(me_r + k, rows_n), me_r).wait_recv()

        for kb in range(BLOCKS):
            start = (t * BLOCKS + kb) * WIDTH
            width = min(WIDTH, depth - start)
            if width <= 0:
                continue
            q = iota((q_dev, LANES), 0)
            source = lax.div(q, q_own) * tall + kb * q_own + lax.rem(q, q_own)
            pick = jnp.where(source == iota((q_dev, LANES), 1), 1.0, 0.0).astype(BF16)
            g = jnp.dot(pick, x_all[t], preferred_element_type=F32).astype(BF16)
            partial = partial + lax.dot_general(
                g[:, :width], t_buf[:, pl.ds(start, width)], NT, preferred_element_type=F32
            )

    cp_w.wait()
    half = jnp.dot(split(partial), w_buf[...], preferred_element_type=F32)
    half = split(half[:q_dev] + half[q_dev:])

    def partial_copy(source, to):
        return pltpu.make_async_remote_copy(
            src_ref=d_buf.at[to],
            dst_ref=r_buf.at[source],
            send_sem=ds.at[to],
            recv_sem=dr.at[source],
            device_id={"col": to, "aux": 1 - me_a},
            device_id_type=MESH,
        )

    quads = cols_n // QUAD
    my_quad = lax.div(me_c, QUAD)
    lower = lax.rem(iota((q_dev // 2, LANES), 1), 2 * TAIL) < TAIL
    for step in range(quads):
        quad = lax.rem(my_quad + (2, 1, 3, 0)[step], quads)
        lanes = QUAD // 2 * pair
        part = spread[:, pl.ds(pl.multiple_of(quad * lanes, lanes), lanes)]
        slots = jnp.dot(half, part, preferred_element_type=F32)
        slots = slots[:q_dev] + slots[q_dev:]
        for j in range(QUAD):
            to = quad * QUAD + j
            first = j // 2 * pair
            head = slots[:, first + j % 2 * LANES : first + (j % 2 + 1) * LANES]
            tail = slots[:, first + 2 * LANES : first + 3 * LANES]
            upper_q, lower_q = tail[: q_dev // 2], tail[q_dev // 2 :]
            if j % 2:
                upper_q = pltpu.roll(upper_q, LANES - TAIL, 1)
            else:
                lower_q = pltpu.roll(lower_q, TAIL, 1)
            d_buf[to, pl.ds(0, q_dev), :] = head
            d_buf[to, pl.ds(q_dev, q_dev // 2), :] = jnp.where(lower, upper_q, lower_q)
            partial_copy(me_c, to).start()

    total = jnp.zeros((dense, LANES), F32)
    for k in (0,) + far[::-1]:
        source = lax.rem(me_c + k, cols_n)
        partial_copy(source, me_c).wait_recv()
        total = total + r_buf[source]
    total = jnp.concatenate([total, jnp.zeros((LANES - dense, LANES), F32)], axis=0)
    z_buf[...] = total.T.astype(BF16)

    def slot_copy(source, to):
        return pltpu.make_async_remote_copy(
            src_ref=z_buf.at[pl.ds(pl.multiple_of(to * HEAD, HEAD), HEAD), :],
            dst_ref=z_all.at[pl.ds(pl.multiple_of(source * HEAD, HEAD), HEAD), :],
            send_sem=zs.at[to],
            recv_sem=zr.at[source],
            device_id={"row": to, "aux": 1 - me_a},
            device_id_type=MESH,
        )

    for k in order + (0,):
        slot_copy(me_r, row_at(k)).start()

    @pl.loop(0, rows_n)
    def _(k):
        slot_copy(row_at(k), me_r).wait_recv()

    got = jnp.concatenate([z_all[pl.ds(i * HEAD, HEAD), :] for i in range(rows_n)], axis=1)
    result = jnp.dot(got, expand[...], preferred_element_type=F32)
    wide = rows_n * q_dev
    tail = jnp.concatenate(
        [result[:TAIL, wide : wide + LANES], result[TAIL:, wide + LANES :]], axis=1
    )
    out[...] = jnp.concatenate([result[:, :wide], tail], axis=0).astype(BF16)

    @pl.loop(1, rows_n)
    def _(k):
        for t in range(chunks):
            panel_copy(t, me_r, row_at(k)).wait_send()

    @pl.loop(0, cols_n)
    def _(to):
        partial_copy(me_c, to).wait_send()

    @pl.loop(0, rows_n)
    def _(to):
        slot_copy(me_r, to).wait_send()


def shards(panels, amplitudes, virt_coeff, row_owner):
    rows_n = lax.axis_size("row")
    cols_n = lax.axis_size("col")
    q_own, depth = panels.shape
    nao, virt = virt_coeff.shape
    q_dev = rows_n * q_own
    chunks = -(-depth // (BLOCKS * WIDTH))
    tall = BLOCKS * q_own
    padded = -(-nao // WIDTH) * WIDTH
    dense = q_dev + q_dev // 2
    vmem = pltpu.VMEM
    dma = pltpu.SemaphoreType.DMA
    return pl.pallas_call(
        functools.partial(kernel, rows_n, cols_n),
        out_shape=pltpu.VMEM((HEAD + TAIL, rows_n * q_dev), BF16),
        in_specs=[pl.BlockSpec(memory_space=pl.ANY)] * 4,
        out_specs=pl.BlockSpec(memory_space=pltpu.VMEM),
        scratch_shapes=[
            vmem(amplitudes.shape, BF16),
            vmem((virt, nao), BF16),
            vmem(panels.shape, BF16),
            vmem((1, nao), jnp.int32),
            vmem((1, padded), jnp.int32),
            vmem((chunks, tall, WIDTH), F32),
            vmem((chunks, rows_n * tall, WIDTH), BF16),
            vmem((padded, LANES), F32),
            vmem((nao, cols_n // 2 * 3 * LANES), BF16),
            vmem((rows_n * LANES, 2 * rows_n * q_dev), BF16),
            vmem((cols_n, dense, LANES), F32),
            vmem((cols_n, dense, LANES), F32),
            vmem((rows_n * HEAD, LANES), BF16),
            vmem((rows_n * HEAD, LANES), BF16),
            dma((4,)),
            dma((chunks, rows_n)),
            dma((chunks, rows_n)),
            dma((cols_n,)),
            dma((cols_n,)),
            dma((rows_n,)),
            dma((rows_n,)),
        ],
        compiler_params=pltpu.CompilerParams(
            collective_id=0, has_side_effects=True, vmem_limit_bytes=56 * 1024 * 1024
        ),
        cost_estimate=pl.CostEstimate(
            flops=2 * virt * depth * LANES, bytes_accessed=amplitudes.size * 2, transcendentals=0
        ),
        name="density",
    )(panels, row_owner.reshape(1, nao), amplitudes, virt_coeff.T)


def solution(mesh):
    placed = (P(("aux", "row"), "col"), P("row", "col"), P(), P())
    return jax.shard_map(
        shards, mesh=mesh, in_specs=placed, out_specs=P(("row", "col"), "aux"), check_vma=False
    )
```

```python
import functools
import jax
import jax.numpy as jnp
from jax import lax
from jax.experimental import pallas as pl
from jax.experimental.pallas import tpu as pltpu
from jax.sharding import PartitionSpec as P

F32 = jnp.float32
BF16 = jnp.bfloat16
MESH = pl.DeviceIdType.MESH
NT = (((1,), (1,)), ((), ()))

LANES = 128
BLOCKS = 4
WIDTH = 256
HEAD = 16
TAIL = 8
QUAD = 4


def split(x):
    hi = x.astype(BF16)
    lo = (x - hi.astype(F32)).astype(BF16)
    return jnp.concatenate([hi, lo], axis=0)


def iota(shape, dim):
    return lax.broadcasted_iota(jnp.int32, shape, dim)


def kernel(
    rows_n,
    cols_n,
    panels,
    owner,
    amp,
    coeff_t,
    out,
    t_buf,
    w_buf,
    p_buf,
    o_buf,
    names,
    x_stage,
    x_all,
    place,
    spread,
    expand,
    d_buf,
    r_buf,
    z_buf,
    z_all,
    local_sem,
    xs,
    xr,
    ds,
    dr,
    zs,
    zr,
):
    me_r = lax.axis_index("row")
    me_c = lax.axis_index("col")
    q_own, depth = panels.shape
    virt, nao = coeff_t.shape
    q_dev = rows_n * q_own
    chunks = x_all.shape[0]
    tall = BLOCKS * q_own
    count = rows_n * cols_n
    dense = q_dev + q_dev // 2
    pair = 3 * LANES
    order = (4, 3, 5, 2, 6, 1, 7)
    far = (10, 6, 9, 11, 5, 7, 8, 2, 14, 13, 15, 12, 4, 3, 1)

    def row_at(k):
        return lax.rem(me_r + k, rows_n)

    barrier = pltpu.get_barrier_semaphore()
    def greet(**to):
        pl.semaphore_signal(barrier, inc=1, device_id=to, device_id_type=MESH)

    for k in order:
        greet(row=row_at(k))
    for k in far:
        greet(col=lax.rem(me_c + k, cols_n))
    cp_p = pltpu.make_async_copy(panels, p_buf, local_sem.at[0])
    cp_o = pltpu.make_async_copy(owner, o_buf, local_sem.at[1])
    cp_t = pltpu.make_async_copy(amp, t_buf, local_sem.at[2])
    cp_w = pltpu.make_async_copy(coeff_t, w_buf, local_sem.at[3])
    cp_p.start()
    cp_o.start()
    cp_t.start()
    cp_w.start()

    x_stage[...] = jnp.zeros_like(x_stage)
    cp_p.wait()
    for t in range(chunks):
        for kb in range(BLOCKS):
            start = (t * BLOCKS + kb) * WIDTH
            width = min(WIDTH, depth - start)
            if width > 0:
                x_stage[t, pl.ds(kb * q_own, q_own), pl.ds(0, width)] = p_buf[
                    :, pl.ds(start, width)
                ].astype(F32)
    own_rows = pl.ds(pl.multiple_of(me_r * tall, tall), tall)
    for t in range(chunks):
        x_all[t, own_rows, :] = x_stage[t].astype(BF16)

    pl.semaphore_wait(barrier, rows_n - 1 + cols_n - 1)

    def panel_copy(t, source, to):
        rows = x_all.at[t, pl.ds(pl.multiple_of(source * tall, tall), tall), :]
        return pltpu.make_async_remote_copy(
            src_ref=rows,
            dst_ref=rows,
            send_sem=xs.at[t, to],
            recv_sem=xr.at[t, source],
            device_id={"row": to},
            device_id_type=MESH,
        )

    for t in range(chunks):
        for k in order:
            panel_copy(t, me_r, row_at(k)).start()

    names[...] = jnp.full_like(names, -1)
    cp_o.wait()
    names[:, pl.ds(0, nao)] = o_buf[...]
    tri = (iota((WIDTH, WIDTH), 0) < iota((WIDTH, WIDTH), 1)).astype(BF16)
    carry = jnp.zeros((count, 1), F32)
    for b in range(names.shape[1] // WIDTH):
        name = names[:, pl.ds(b * WIDTH, WIDTH)]
        ones = jnp.where(name == iota((count, WIDTH), 0), 1.0, 0.0).astype(F32)
        before = jnp.dot(ones.astype(BF16), tri, preferred_element_type=F32) + carry
        slot = jnp.sum(ones * before, axis=0, keepdims=True)
        carry = carry + jnp.sum(ones, axis=1, keepdims=True)
        at_row = lax.div(name, jnp.int32(cols_n))
        at_col = name - at_row * cols_n
        at_pair = lax.div(at_col, jnp.int32(2))
        odd = at_col - at_pair * 2
        base = (at_pair * pair + at_row * HEAD).astype(F32)
        early = base + (odd * LANES).astype(F32) + slot
        late = base + (odd * TAIL + (2 * LANES - HEAD)).astype(F32) + slot
        lane = jnp.where(slot < HEAD, early, late)
        lane = jnp.where(name < 0, -1.0, lane)
        place[pl.ds(b * WIDTH, WIDTH), :] = jnp.broadcast_to(lane, (LANES, WIDTH)).T

    @pl.loop(0, spread.shape[1] // LANES)
    def _(b):
        at = (iota((nao, LANES), 1) + b * LANES).astype(F32)
        hot = jnp.where(place[pl.ds(0, nao), :] == at, 1.0, 0.0)
        spread[:, pl.ds(pl.multiple_of(b * LANES, LANES), LANES)] = hot.astype(BF16)

    for i in range(rows_n):
        a = iota((LANES, rows_n * q_dev), 0)
        n = iota((LANES, rows_n * q_dev), 1)
        head = jnp.where((a < q_dev) & (n == a * rows_n + i), 1.0, 0.0)
        tail = jnp.where(
            (a >= q_dev) & (a < dense) & (lax.rem(n, LANES) == (a - q_dev) * rows_n + i), 1.0, 0.0
        )
        expand[pl.ds(i * LANES, LANES), :] = jnp.concatenate([head, tail], axis=1).astype(BF16)

    cp_t.wait()
    partial = jnp.zeros((q_dev, virt), F32)
    for t in range(chunks):

        @pl.loop(1, rows_n)
        def _(k):
            panel_copy(t, lax.rem(me_r + k, rows_n), me_r).wait_recv()

        for kb in range(BLOCKS):
            start = (t * BLOCKS + kb) * WIDTH
            width = min(WIDTH, depth - start)
            if width <= 0:
                continue
            q = iota((q_dev, LANES), 0)
            source = lax.div(q, q_own) * tall + kb * q_own + lax.rem(q, q_own)
            pick = jnp.where(source == iota((q_dev, LANES), 1), 1.0, 0.0).astype(BF16)
            g = jnp.dot(pick, x_all[t], preferred_element_type=F32).astype(BF16)
            partial = partial + lax.dot_general(
                g[:, :width], t_buf[:, pl.ds(start, width)], NT, preferred_element_type=F32
            )

    cp_w.wait()
    half = jnp.dot(split(partial), w_buf[...], preferred_element_type=F32)
    half = split(half[:q_dev] + half[q_dev:])

    def partial_copy(source, to):
        return pltpu.make_async_remote_copy(
            src_ref=d_buf.at[to],
            dst_ref=r_buf.at[source],
            send_sem=ds.at[to],
            recv_sem=dr.at[source],
            device_id={"col": to},
            device_id_type=MESH,
        )

    quads = cols_n // QUAD
    my_quad = lax.div(me_c, QUAD)
    lower = lax.rem(iota((q_dev // 2, LANES), 1), 2 * TAIL) < TAIL
    for step in range(quads):
        quad = lax.rem(my_quad + (2, 1, 3, 0)[step], quads)
        lanes = QUAD // 2 * pair
        part = spread[:, pl.ds(pl.multiple_of(quad * lanes, lanes), lanes)]
        slots = jnp.dot(half, part, preferred_element_type=F32)
        slots = slots[:q_dev] + slots[q_dev:]
        for j in range(QUAD):
            to = quad * QUAD + j
            first = j // 2 * pair
            head = slots[:, first + j % 2 * LANES : first + (j % 2 + 1) * LANES]
            tail = slots[:, first + 2 * LANES : first + 3 * LANES]
            upper_q, lower_q = tail[: q_dev // 2], tail[q_dev // 2 :]
            if j % 2:
                upper_q = pltpu.roll(upper_q, LANES - TAIL, 1)
            else:
                lower_q = pltpu.roll(lower_q, TAIL, 1)
            d_buf[to, pl.ds(0, q_dev), :] = head
            d_buf[to, pl.ds(q_dev, q_dev // 2), :] = jnp.where(lower, upper_q, lower_q)
        for k in (2, 1, 3, 0):
            to = quad * QUAD + lax.rem(me_c + k, QUAD)
            if step < quads - 1 or k:
                partial_copy(me_c, to).start()

    total = d_buf[me_c]
    for k in far[::-1]:
        source = lax.rem(me_c + k, cols_n)
        partial_copy(source, me_c).wait_recv()
        total = total + r_buf[source]
    total = jnp.concatenate([total, jnp.zeros((LANES - dense, LANES), F32)], axis=0)
    z_buf[...] = total.T.astype(BF16)

    def slot_copy(source, to):
        return pltpu.make_async_remote_copy(
            src_ref=z_buf.at[pl.ds(pl.multiple_of(to * HEAD, HEAD), HEAD), :],
            dst_ref=z_all.at[pl.ds(pl.multiple_of(source * HEAD, HEAD), HEAD), :],
            send_sem=zs.at[to],
            recv_sem=zr.at[source],
            device_id={"row": to},
            device_id_type=MESH,
        )

    for k in order:
        slot_copy(me_r, row_at(k)).start()
    own = pl.ds(pl.multiple_of(me_r * HEAD, HEAD), HEAD)
    z_all[own, :] = z_buf[own, :]

    @pl.loop(1, rows_n)
    def _(k):
        slot_copy(row_at(k), me_r).wait_recv()

    got = jnp.concatenate([z_all[pl.ds(i * HEAD, HEAD), :] for i in range(rows_n)], axis=1)
    result = jnp.dot(got, expand[...], preferred_element_type=F32)
    wide = rows_n * q_dev
    tail = jnp.concatenate(
        [result[:TAIL, wide : wide + LANES], result[TAIL:, wide + LANES :]], axis=1
    )
    out[...] = jnp.concatenate([result[:, :wide], tail], axis=0).astype(BF16)

    @pl.loop(1, rows_n)
    def _(k):
        for t in range(chunks):
            panel_copy(t, me_r, row_at(k)).wait_send()
        slot_copy(me_r, row_at(k)).wait_send()

    @pl.loop(1, cols_n)
    def _(k):
        partial_copy(me_c, lax.rem(me_c + k, cols_n)).wait_send()


def shards(panels, amplitudes, virt_coeff, row_owner):
    rows_n = lax.axis_size("row")
    cols_n = lax.axis_size("col")
    q_own, depth = panels.shape
    nao, virt = virt_coeff.shape
    q_dev = rows_n * q_own
    chunks = -(-depth // (BLOCKS * WIDTH))
    tall = BLOCKS * q_own
    padded = -(-nao // WIDTH) * WIDTH
    dense = q_dev + q_dev // 2
    vmem = pltpu.VMEM
    dma = pltpu.SemaphoreType.DMA
    return pl.pallas_call(
        functools.partial(kernel, rows_n, cols_n),
        out_shape=pltpu.VMEM((HEAD + TAIL, rows_n * q_dev), BF16),
        in_specs=[pl.BlockSpec(memory_space=pl.ANY)] * 4,
        out_specs=pl.BlockSpec(memory_space=pltpu.VMEM),
        scratch_shapes=[
            vmem(amplitudes.shape, BF16),
            vmem((virt, nao), BF16),
            vmem(panels.shape, BF16),
            vmem((1, nao), jnp.int32),
            vmem((1, padded), jnp.int32),
            vmem((chunks, tall, WIDTH), F32),
            vmem((chunks, rows_n * tall, WIDTH), BF16),
            vmem((padded, LANES), F32),
            vmem((nao, cols_n // 2 * 3 * LANES), BF16),
            vmem((rows_n * LANES, 2 * rows_n * q_dev), BF16),
            vmem((cols_n, dense, LANES), F32),
            vmem((cols_n, dense, LANES), F32),
            vmem((rows_n * HEAD, LANES), BF16),
            vmem((rows_n * HEAD, LANES), BF16),
            dma((4,)),
            dma((chunks, rows_n)),
            dma((chunks, rows_n)),
            dma((cols_n,)),
            dma((cols_n,)),
            dma((rows_n,)),
            dma((rows_n,)),
        ],
        compiler_params=pltpu.CompilerParams(
            collective_id=0, has_side_effects=True, vmem_limit_bytes=56 * 1024 * 1024
        ),
        cost_estimate=pl.CostEstimate(
            flops=2 * virt * depth * LANES, bytes_accessed=amplitudes.size * 2, transcendentals=0
        ),
        name="density",
    )(panels, row_owner.reshape(1, nao), amplitudes, virt_coeff.T)


def solution(mesh):
    placed = (P(("aux", "row"), "col"), P("row", "col"), P(), P())
    return jax.shard_map(
        shards, mesh=mesh, in_specs=placed, out_specs=P(("row", "col"), "aux"), check_vma=False
    )
```

```python
import functools
import jax
import jax.numpy as jnp
from jax import lax
from jax.experimental import pallas as pl
from jax.experimental.pallas import tpu as pltpu
from jax.sharding import PartitionSpec as P

F32 = jnp.float32
BF16 = jnp.bfloat16
MESH = pl.DeviceIdType.MESH

LANES = 128
BLOCKS = 4
WIDTH = 256
HEAD = 16
TAIL = 8
QUAD = 4


def split(x):
    hi = x.astype(BF16)
    lo = (x - hi.astype(F32)).astype(BF16)
    return jnp.concatenate([hi, lo], axis=0)


def iota(shape, dim):
    return lax.broadcasted_iota(jnp.int32, shape, dim)


def kernel(
    rows_n,
    cols_n,
    panels,
    owner,
    amp,
    coeff_t,
    out,
    t_buf,
    tt_buf,
    w_buf,
    p_buf,
    o_buf,
    names,
    x_stage,
    x_all,
    place,
    spread,
    expand,
    d_buf,
    r_buf,
    z_buf,
    z_all,
    local_sem,
    xs,
    xr,
    ds,
    dr,
    zs,
    zr,
):
    me_r = lax.axis_index("row")
    me_c = lax.axis_index("col")
    q_own, depth = panels.shape
    virt, nao = coeff_t.shape
    q_dev = rows_n * q_own
    chunks = x_all.shape[0]
    tall = BLOCKS * q_own
    count = rows_n * cols_n
    dense = q_dev + q_dev // 2
    pair = 3 * LANES
    order = (4, 3, 5, 2, 6, 1, 7)
    far = (10, 6, 9, 11, 5, 7, 8, 2, 14, 13, 15, 12, 4, 3, 1)

    def row_at(k):
        return lax.rem(me_r + k, rows_n)

    barrier = pltpu.get_barrier_semaphore()
    def greet(**to):
        pl.semaphore_signal(barrier, inc=1, device_id=to, device_id_type=MESH)

    for k in order:
        greet(row=row_at(k))
    cp_p = pltpu.make_async_copy(panels, p_buf, local_sem.at[0])
    cp_o = pltpu.make_async_copy(owner, o_buf, local_sem.at[1])
    cp_t = pltpu.make_async_copy(amp, t_buf, local_sem.at[2])
    cp_w = pltpu.make_async_copy(coeff_t, w_buf, local_sem.at[3])
    cp_p.start()
    cp_o.start()
    cp_t.start()
    for k in far:
        greet(col=lax.rem(me_c + k, cols_n))

    names[...] = jnp.full_like(names, -1)
    cp_o.wait()
    names[:, pl.ds(0, nao)] = o_buf[...]
    tri = (iota((WIDTH, WIDTH), 0) < iota((WIDTH, WIDTH), 1)).astype(BF16)
    carry = jnp.zeros((count, 1), F32)
    for b in range(names.shape[1] // WIDTH):
        name = names[:, pl.ds(b * WIDTH, WIDTH)]
        ones = jnp.where(name == iota((count, WIDTH), 0), 1.0, 0.0).astype(F32)
        before = jnp.dot(ones.astype(BF16), tri, preferred_element_type=F32) + carry
        slot = jnp.sum(ones * before, axis=0, keepdims=True)
        carry = carry + jnp.sum(ones, axis=1, keepdims=True)
        at_row = lax.div(name, jnp.int32(cols_n))
        at_col = name - at_row * cols_n
        at_pair = lax.div(at_col, jnp.int32(2))
        odd = at_col - at_pair * 2
        base = (at_pair * pair + at_row * HEAD).astype(F32)
        early = base + (odd * LANES).astype(F32) + slot
        late = base + (odd * TAIL + (2 * LANES - HEAD)).astype(F32) + slot
        lane = jnp.where(slot < HEAD, early, late)
        lane = jnp.where(name < 0, -1.0, lane)
        place[pl.ds(b * WIDTH, WIDTH), :] = jnp.broadcast_to(lane, (LANES, WIDTH)).T

    @pl.loop(0, spread.shape[1] // LANES)
    def _(b):
        at = (iota((nao, LANES), 1) + b * LANES).astype(F32)
        hot = jnp.where(place[pl.ds(0, nao), :] == at, 1.0, 0.0)
        spread[:, pl.ds(pl.multiple_of(b * LANES, LANES), LANES)] = hot.astype(BF16)

    x_stage[...] = jnp.zeros_like(x_stage)
    cp_p.wait()
    for t in range(chunks):
        for kb in range(BLOCKS):
            start = (t * BLOCKS + kb) * WIDTH
            width = min(WIDTH, depth - start)
            if width > 0:
                x_stage[t, pl.ds(kb * q_own, q_own), pl.ds(0, width)] = p_buf[
                    :, pl.ds(start, width)
                ].astype(F32)
    own_rows = pl.ds(pl.multiple_of(me_r * tall, tall), tall)
    for t in range(chunks):
        x_all[t, own_rows, :] = x_stage[t].astype(BF16)

    pl.semaphore_wait(barrier, rows_n - 1 + cols_n - 1)

    def panel_copy(t, source, to):
        rows = x_all.at[t, pl.ds(pl.multiple_of(source * tall, tall), tall), :]
        return pltpu.make_async_remote_copy(
            src_ref=rows,
            dst_ref=rows,
            send_sem=xs.at[t],
            recv_sem=xr.at[t],
            device_id={"row": to},
            device_id_type=MESH,
        )

    for t in range(chunks):
        for k in order:
            panel_copy(t, me_r, row_at(k)).start()

    cp_t.wait()
    cp_w.start()
    for k in range(0, depth, WIDTH):
        width = min(WIDTH, depth - k)
        tt_buf[pl.ds(k, width), :] = t_buf[:, pl.ds(k, width)].T

    for i in range(rows_n):
        a = iota((LANES, rows_n * q_dev), 0)
        n = iota((LANES, rows_n * q_dev), 1)
        head = jnp.where((a < q_dev) & (n == a * rows_n + i), 1.0, 0.0)
        tail = jnp.where(
            (a >= q_dev) & (a < dense) & (lax.rem(n, LANES) == (a - q_dev) * rows_n + i), 1.0, 0.0
        )
        expand[pl.ds(i * LANES, LANES), :] = jnp.concatenate([head, tail], axis=1).astype(BF16)

    partial = jnp.zeros((q_dev, virt), F32)
    for t in range(chunks):
        others = x_all.at[t, pl.ds(0, (rows_n - 1) * tall), :]
        pltpu.make_async_copy(others, others, xr.at[t]).wait()
        for kb in range(BLOCKS):
            start = (t * BLOCKS + kb) * WIDTH
            width = min(WIDTH, depth - start)
            if width <= 0:
                continue
            q = iota((q_dev, LANES), 0)
            source = lax.div(q, q_own) * tall + kb * q_own + lax.rem(q, q_own)
            pick = jnp.where(source == iota((q_dev, LANES), 1), 1.0, 0.0).astype(BF16)
            g = jnp.dot(pick, x_all[t], preferred_element_type=F32).astype(BF16)
            partial = partial + jnp.dot(
                g[:, :width], tt_buf[pl.ds(start, width), :], preferred_element_type=F32
            )

    cp_w.wait()
    half = jnp.dot(split(partial), w_buf[...], preferred_element_type=F32)
    half = split(half[:q_dev] + half[q_dev:])

    def partial_copy(source, to):
        return pltpu.make_async_remote_copy(
            src_ref=d_buf.at[to],
            dst_ref=r_buf.at[source],
            send_sem=ds.at[0],
            recv_sem=dr.at[0],
            device_id={"col": to},
            device_id_type=MESH,
        )

    quads = cols_n // QUAD
    my_quad = lax.div(me_c, QUAD)
    lower = lax.rem(iota((q_dev // 2, LANES), 1), 2 * TAIL) < TAIL
    for step in range(quads):
        quad = lax.rem(my_quad + (2, 1, 3, 0)[step], quads)
        lanes = QUAD // 2 * pair
        part = spread[:, pl.ds(pl.multiple_of(quad * lanes, lanes), lanes)]
        slots = jnp.dot(half, part, preferred_element_type=F32)
        slots = slots[:q_dev] + slots[q_dev:]
        for j in range(QUAD):
            to = quad * QUAD + j
            first = j // 2 * pair
            head = slots[:, first + j % 2 * LANES : first + (j % 2 + 1) * LANES]
            tail = slots[:, first + 2 * LANES : first + 3 * LANES]
            upper_q, lower_q = tail[: q_dev // 2], tail[q_dev // 2 :]
            if j % 2:
                upper_q = pltpu.roll(upper_q, LANES - TAIL, 1)
            else:
                lower_q = pltpu.roll(lower_q, TAIL, 1)
            d_buf[to, pl.ds(0, q_dev), :] = head
            d_buf[to, pl.ds(q_dev, q_dev // 2), :] = jnp.where(lower, upper_q, lower_q)
        for k in (2, 1, 3, 0):
            to = quad * QUAD + lax.rem(me_c + k, QUAD)
            if step < quads - 1 or k:
                partial_copy(me_c, to).start()

    for t in range(chunks):
        sent = x_all.at[t, pl.ds(0, (rows_n - 1) * tall), :]
        pltpu.make_async_copy(sent, sent, xs.at[t]).wait()
    others = r_buf.at[pl.ds(0, cols_n - 1)]
    pltpu.make_async_copy(others, others, dr.at[0]).wait()
    total = d_buf[me_c]
    for k in range(1, cols_n):
        total = total + r_buf[lax.rem(me_c + k, cols_n)]
    total = jnp.concatenate([total, jnp.zeros((LANES - dense, LANES), F32)], axis=0)
    z_buf[...] = total.T.astype(BF16)

    def slot_copy(source, to):
        return pltpu.make_async_remote_copy(
            src_ref=z_buf.at[pl.ds(pl.multiple_of(to * HEAD, HEAD), HEAD), :],
            dst_ref=z_all.at[pl.ds(pl.multiple_of(source * HEAD, HEAD), HEAD), :],
            send_sem=zs.at[0],
            recv_sem=zr.at[0],
            device_id={"row": to},
            device_id_type=MESH,
        )

    for k in order:
        slot_copy(me_r, row_at(k)).start()
    own = pl.ds(pl.multiple_of(me_r * HEAD, HEAD), HEAD)
    z_all[own, :] = z_buf[own, :]

    partials_sent = d_buf.at[pl.ds(0, cols_n - 1)]
    pltpu.make_async_copy(partials_sent, partials_sent, ds.at[0]).wait()

    others = z_all.at[pl.ds(0, (rows_n - 1) * HEAD), :]
    pltpu.make_async_copy(others, others, zr.at[0]).wait()

    got = jnp.concatenate([z_all[pl.ds(i * HEAD, HEAD), :] for i in range(rows_n)], axis=1)
    result = jnp.dot(got, expand[...], preferred_element_type=F32)
    wide = rows_n * q_dev
    tail = jnp.concatenate(
        [result[:TAIL, wide : wide + LANES], result[TAIL:, wide + LANES :]], axis=1
    )
    out[...] = jnp.concatenate([result[:, :wide], tail], axis=0).astype(BF16)

    slots_sent = z_buf.at[pl.ds(0, (rows_n - 1) * HEAD), :]
    pltpu.make_async_copy(slots_sent, slots_sent, zs.at[0]).wait()


def shards(panels, amplitudes, virt_coeff, row_owner):
    rows_n = lax.axis_size("row")
    cols_n = lax.axis_size("col")
    q_own, depth = panels.shape
    nao, virt = virt_coeff.shape
    q_dev = rows_n * q_own
    chunks = -(-depth // (BLOCKS * WIDTH))
    tall = BLOCKS * q_own
    padded = -(-nao // WIDTH) * WIDTH
    dense = q_dev + q_dev // 2
    vmem = pltpu.VMEM
    dma = pltpu.SemaphoreType.DMA
    return pl.pallas_call(
        functools.partial(kernel, rows_n, cols_n),
        out_shape=pltpu.VMEM((HEAD + TAIL, rows_n * q_dev), BF16),
        in_specs=[pl.BlockSpec(memory_space=pl.ANY)] * 4,
        out_specs=pl.BlockSpec(memory_space=pltpu.VMEM),
        scratch_shapes=[
            vmem(amplitudes.shape, BF16),
            vmem((depth, virt), BF16),
            vmem((virt, nao), BF16),
            vmem(panels.shape, BF16),
            vmem((1, nao), jnp.int32),
            vmem((1, padded), jnp.int32),
            vmem((chunks, tall, WIDTH), F32),
            vmem((chunks, rows_n * tall, WIDTH), BF16),
            vmem((padded, LANES), F32),
            vmem((nao, cols_n // 2 * 3 * LANES), BF16),
            vmem((rows_n * LANES, 2 * rows_n * q_dev), BF16),
            vmem((cols_n, dense, LANES), F32),
            vmem((cols_n, dense, LANES), F32),
            vmem((rows_n * HEAD, LANES), BF16),
            vmem((rows_n * HEAD, LANES), BF16),
            dma((4,)),
            dma((chunks,)),
            dma((chunks,)),
            dma((1,)),
            dma((1,)),
            dma((1,)),
            dma((1,)),
        ],
        compiler_params=pltpu.CompilerParams(
            collective_id=0, has_side_effects=True, vmem_limit_bytes=56 * 1024 * 1024
        ),
        cost_estimate=pl.CostEstimate(
            flops=2 * virt * depth * LANES, bytes_accessed=amplitudes.size * 2, transcendentals=0
        ),
        name="density",
    )(panels, row_owner.reshape(1, nao), amplitudes, virt_coeff.T)


def solution(mesh):
    placed = (P(("aux", "row"), "col"), P("row", "col"), P(), P())
    return jax.shard_map(
        shards, mesh=mesh, in_specs=placed, out_specs=P(("row", "col"), "aux"), check_vma=False
    )
```

```python
import functools
import jax
import jax.numpy as jnp
from jax import lax
from jax.experimental import pallas as pl
from jax.experimental.pallas import tpu as pltpu
from jax.sharding import PartitionSpec as P

F32 = jnp.float32
BF16 = jnp.bfloat16
MESH = pl.DeviceIdType.MESH
NT = (((1,), (1,)), ((), ()))

LANES = 128
BLOCKS = 4
WIDTH = 256
HEAD = 16
TAIL = 8
QUAD = 4


def split(x):
    hi = x.astype(BF16)
    lo = (x - hi.astype(F32)).astype(BF16)
    return jnp.concatenate([hi, lo], axis=0)


def iota(shape, dim):
    return lax.broadcasted_iota(jnp.int32, shape, dim)


def kernel(
    rows_n,
    cols_n,
    panels,
    owner,
    amp,
    coeff_t,
    out,
    t_buf,
    w_buf,
    p_buf,
    o_buf,
    names,
    x_stage,
    x_all,
    place,
    spread,
    expand,
    d_buf,
    r_buf,
    z_buf,
    z_all,
    local_sem,
    xs,
    xr,
    ds,
    dr,
    zs,
    zr,
):
    me_r = lax.axis_index("row")
    me_c = lax.axis_index("col")
    q_own, depth = panels.shape
    virt, nao = coeff_t.shape
    q_dev = rows_n * q_own
    chunks = x_all.shape[0]
    tall = BLOCKS * q_own
    count = rows_n * cols_n
    dense = q_dev + q_dev // 2
    pair = 3 * LANES
    order = (4, 3, 5, 2, 6, 1, 7)
    far = (10, 6, 9, 11, 5, 7, 8, 2, 14, 13, 15, 12, 4, 3, 1)

    def row_at(k):
        return lax.rem(me_r + k, rows_n)

    barrier = pltpu.get_barrier_semaphore()
    def greet(**to):
        pl.semaphore_signal(barrier, inc=1, device_id=to, device_id_type=MESH)

    for k in order:
        greet(row=row_at(k))
    cp_p = pltpu.make_async_copy(panels, p_buf, local_sem.at[0])
    cp_o = pltpu.make_async_copy(owner, o_buf, local_sem.at[1])
    cp_t = pltpu.make_async_copy(amp, t_buf, local_sem.at[2])
    cp_w = pltpu.make_async_copy(coeff_t, w_buf, local_sem.at[3])
    cp_p.start()
    cp_o.start()
    cp_t.start()
    cp_w.start()
    for k in far:
        greet(col=lax.rem(me_c + k, cols_n))

    x_stage[...] = jnp.zeros_like(x_stage)
    cp_p.wait()
    for t in range(chunks):
        for kb in range(BLOCKS):
            start = (t * BLOCKS + kb) * WIDTH
            width = min(WIDTH, depth - start)
            if width > 0:
                x_stage[t, pl.ds(kb * q_own, q_own), pl.ds(0, width)] = p_buf[
                    :, pl.ds(start, width)
                ].astype(F32)
    own_rows = pl.ds(pl.multiple_of(me_r * tall, tall), tall)
    for t in range(chunks):
        x_all[t, own_rows, :] = x_stage[t].astype(BF16)

    pl.semaphore_wait(barrier, rows_n - 1 + cols_n - 1)

    def panel_copy(t, source, to):
        rows = x_all.at[t, pl.ds(pl.multiple_of(source * tall, tall), tall), :]
        return pltpu.make_async_remote_copy(
            src_ref=rows,
            dst_ref=rows,
            send_sem=xs.at[t],
            recv_sem=xr.at[t],
            device_id={"row": to},
            device_id_type=MESH,
        )

    for t in range(chunks):
        for k in order:
            panel_copy(t, me_r, row_at(k)).start()

    names[...] = jnp.full_like(names, -1)
    cp_o.wait()
    names[:, pl.ds(0, nao)] = o_buf[...]
    tri = (iota((WIDTH, WIDTH), 0) < iota((WIDTH, WIDTH), 1)).astype(BF16)
    carry = jnp.zeros((count, 1), F32)
    for b in range(names.shape[1] // WIDTH):
        name = names[:, pl.ds(b * WIDTH, WIDTH)]
        ones = jnp.where(name == iota((count, WIDTH), 0), 1.0, 0.0).astype(F32)
        before = jnp.dot(ones.astype(BF16), tri, preferred_element_type=F32) + carry
        slot = jnp.sum(ones * before, axis=0, keepdims=True)
        carry = carry + jnp.sum(ones, axis=1, keepdims=True)
        at_row = lax.div(name, jnp.int32(cols_n))
        at_col = name - at_row * cols_n
        at_pair = lax.div(at_col, jnp.int32(2))
        odd = at_col - at_pair * 2
        base = (at_pair * pair + at_row * HEAD).astype(F32)
        early = base + (odd * LANES).astype(F32) + slot
        late = base + (odd * TAIL + (2 * LANES - HEAD)).astype(F32) + slot
        lane = jnp.where(slot < HEAD, early, late)
        lane = jnp.where(name < 0, -1.0, lane)
        place[pl.ds(b * WIDTH, WIDTH), :] = jnp.broadcast_to(lane, (LANES, WIDTH)).T

    @pl.loop(0, spread.shape[1] // LANES)
    def _(b):
        at = (iota((nao, LANES), 1) + b * LANES).astype(F32)
        hot = jnp.where(place[pl.ds(0, nao), :] == at, 1.0, 0.0)
        spread[:, pl.ds(pl.multiple_of(b * LANES, LANES), LANES)] = hot.astype(BF16)

    for i in range(rows_n):
        a = iota((LANES, rows_n * q_dev), 0)
        n = iota((LANES, rows_n * q_dev), 1)
        head = jnp.where((a < q_dev) & (n == a * rows_n + i), 1.0, 0.0)
        tail = jnp.where(
            (a >= q_dev) & (a < dense) & (lax.rem(n, LANES) == (a - q_dev) * rows_n + i), 1.0, 0.0
        )
        expand[pl.ds(i * LANES, LANES), :] = jnp.concatenate([head, tail], axis=1).astype(BF16)

    cp_t.wait()
    partial = jnp.zeros((q_dev, virt), F32)
    for t in range(chunks):
        others = x_all.at[t, pl.ds(0, (rows_n - 1) * tall), :]
        pltpu.make_async_copy(others, others, xr.at[t]).wait()
        for kb in range(BLOCKS):
            start = (t * BLOCKS + kb) * WIDTH
            width = min(WIDTH, depth - start)
            if width <= 0:
                continue
            q = iota((q_dev, LANES), 0)
            source = lax.div(q, q_own) * tall + kb * q_own + lax.rem(q, q_own)
            pick = jnp.where(source == iota((q_dev, LANES), 1), 1.0, 0.0).astype(BF16)
            g = jnp.dot(pick, x_all[t], preferred_element_type=F32).astype(BF16)
            partial = partial + lax.dot_general(
                g[:, :width], t_buf[:, pl.ds(start, width)], NT, preferred_element_type=F32
            )

    cp_w.wait()
    half = jnp.dot(split(partial), w_buf[...], preferred_element_type=F32)
    half = split(half[:q_dev] + half[q_dev:])

    def partial_copy(source, to):
        return pltpu.make_async_remote_copy(
            src_ref=d_buf.at[to],
            dst_ref=r_buf.at[source],
            send_sem=ds.at[0],
            recv_sem=dr.at[0],
            device_id={"col": to},
            device_id_type=MESH,
        )

    quads = cols_n // QUAD
    my_quad = lax.div(me_c, QUAD)
    lower = lax.rem(iota((q_dev // 2, LANES), 1), 2 * TAIL) < TAIL
    for step in range(quads):
        quad = lax.rem(my_quad + (2, 1, 3, 0)[step], quads)
        lanes = QUAD // 2 * pair
        part = spread[:, pl.ds(pl.multiple_of(quad * lanes, lanes), lanes)]
        slots = jnp.dot(half, part, preferred_element_type=F32)
        slots = slots[:q_dev] + slots[q_dev:]
        for j in range(QUAD):
            to = quad * QUAD + j
            first = j // 2 * pair
            head = slots[:, first + j % 2 * LANES : first + (j % 2 + 1) * LANES]
            tail = slots[:, first + 2 * LANES : first + 3 * LANES]
            upper_q, lower_q = tail[: q_dev // 2], tail[q_dev // 2 :]
            if j % 2:
                upper_q = pltpu.roll(upper_q, LANES - TAIL, 1)
            else:
                lower_q = pltpu.roll(lower_q, TAIL, 1)
            d_buf[to, pl.ds(0, q_dev), :] = head
            d_buf[to, pl.ds(q_dev, q_dev // 2), :] = jnp.where(lower, upper_q, lower_q)
        for k in (2, 1, 3, 0):
            to = quad * QUAD + lax.rem(me_c + k, QUAD)
            if step < quads - 1 or k:
                partial_copy(me_c, to).start()

    for t in range(chunks):
        sent = x_all.at[t, pl.ds(0, (rows_n - 1) * tall), :]
        pltpu.make_async_copy(sent, sent, xs.at[t]).wait()
    others = r_buf.at[pl.ds(0, cols_n - 1)]
    pltpu.make_async_copy(others, others, dr.at[0]).wait()
    total = d_buf[me_c]
    for k in range(1, cols_n):
        total = total + r_buf[lax.rem(me_c + k, cols_n)]
    total = jnp.concatenate([total, jnp.zeros((LANES - dense, LANES), F32)], axis=0)
    z_buf[...] = total.T.astype(BF16)

    def slot_copy(source, to):
        return pltpu.make_async_remote_copy(
            src_ref=z_buf.at[pl.ds(pl.multiple_of(to * HEAD, HEAD), HEAD), :],
            dst_ref=z_all.at[pl.ds(pl.multiple_of(source * HEAD, HEAD), HEAD), :],
            send_sem=zs.at[0],
            recv_sem=zr.at[0],
            device_id={"row": to},
            device_id_type=MESH,
        )

    for k in order:
        slot_copy(me_r, row_at(k)).start()
    own = pl.ds(pl.multiple_of(me_r * HEAD, HEAD), HEAD)
    z_all[own, :] = z_buf[own, :]

    partials_sent = d_buf.at[pl.ds(0, cols_n - 1)]
    pltpu.make_async_copy(partials_sent, partials_sent, ds.at[0]).wait()

    others = z_all.at[pl.ds(0, (rows_n - 1) * HEAD), :]
    pltpu.make_async_copy(others, others, zr.at[0]).wait()

    got = jnp.concatenate([z_all[pl.ds(i * HEAD, HEAD), :] for i in range(rows_n)], axis=1)
    result = jnp.dot(got, expand[...], preferred_element_type=F32)
    wide = rows_n * q_dev
    tail = jnp.concatenate(
        [result[:TAIL, wide : wide + LANES], result[TAIL:, wide + LANES :]], axis=1
    )
    out[...] = jnp.concatenate([result[:, :wide], tail], axis=0).astype(BF16)

    slots_sent = z_buf.at[pl.ds(0, (rows_n - 1) * HEAD), :]
    pltpu.make_async_copy(slots_sent, slots_sent, zs.at[0]).wait()


def shards(panels, amplitudes, virt_coeff, row_owner):
    rows_n = lax.axis_size("row")
    cols_n = lax.axis_size("col")
    q_own, depth = panels.shape
    nao, virt = virt_coeff.shape
    q_dev = rows_n * q_own
    chunks = -(-depth // (BLOCKS * WIDTH))
    tall = BLOCKS * q_own
    padded = -(-nao // WIDTH) * WIDTH
    dense = q_dev + q_dev // 2
    vmem = pltpu.VMEM
    dma = pltpu.SemaphoreType.DMA
    return pl.pallas_call(
        functools.partial(kernel, rows_n, cols_n),
        out_shape=pltpu.VMEM((HEAD + TAIL, rows_n * q_dev), BF16),
        in_specs=[pl.BlockSpec(memory_space=pl.ANY)] * 4,
        out_specs=pl.BlockSpec(memory_space=pltpu.VMEM),
        scratch_shapes=[
            vmem(amplitudes.shape, BF16),
            vmem((virt, nao), BF16),
            vmem(panels.shape, BF16),
            vmem((1, nao), jnp.int32),
            vmem((1, padded), jnp.int32),
            vmem((chunks, tall, WIDTH), F32),
            vmem((chunks, rows_n * tall, WIDTH), BF16),
            vmem((padded, LANES), F32),
            vmem((nao, cols_n // 2 * 3 * LANES), BF16),
            vmem((rows_n * LANES, 2 * rows_n * q_dev), BF16),
            vmem((cols_n, dense, LANES), F32),
            vmem((cols_n, dense, LANES), F32),
            vmem((rows_n * HEAD, LANES), BF16),
            vmem((rows_n * HEAD, LANES), BF16),
            dma((4,)),
            dma((chunks,)),
            dma((chunks,)),
            dma((1,)),
            dma((1,)),
            dma((1,)),
            dma((1,)),
        ],
        compiler_params=pltpu.CompilerParams(
            collective_id=0, has_side_effects=True, vmem_limit_bytes=56 * 1024 * 1024
        ),
        cost_estimate=pl.CostEstimate(
            flops=2 * virt * depth * LANES, bytes_accessed=amplitudes.size * 2, transcendentals=0
        ),
        name="density",
    )(panels, row_owner.reshape(1, nao), amplitudes, virt_coeff.T)


def solution(mesh):
    placed = (P(("aux", "row"), "col"), P("row", "col"), P(), P())
    return jax.shard_map(
        shards, mesh=mesh, in_specs=placed, out_specs=P(("row", "col"), "aux"), check_vma=False
    )
```

```python
import functools
import jax
import jax.numpy as jnp
from jax import lax
from jax.experimental import pallas as pl
from jax.experimental.pallas import tpu as pltpu
from jax.sharding import PartitionSpec as P

F32 = jnp.float32
BF16 = jnp.bfloat16
MESH = pl.DeviceIdType.MESH
NT = (((1,), (1,)), ((), ()))

LANES = 128
BLOCKS = 4
WIDTH = 256
HEAD = 16
TAIL = 8
QUAD = 4


def split(x):
    hi = x.astype(BF16)
    lo = (x - hi.astype(F32)).astype(BF16)
    return jnp.concatenate([hi, lo], axis=0)


def iota(shape, dim):
    return lax.broadcasted_iota(jnp.int32, shape, dim)


def kernel(
    rows_n,
    cols_n,
    aux_n,
    panels,
    owner,
    amp,
    coeff_t,
    out,
    t_buf,
    w_buf,
    p_buf,
    o_buf,
    names,
    x_stage,
    x_all,
    place,
    spread,
    expand,
    d_buf,
    r_buf,
    z_buf,
    z_all,
    local_sem,
    xs,
    xr,
    ds,
    dr,
    zs,
    zr,
):
    me_r = lax.axis_index("row")
    me_c = lax.axis_index("col")
    me_a = lax.axis_index("aux")
    hub = aux_n - 1
    summing = me_a == hub
    q_own, depth = panels.shape
    virt, nao = coeff_t.shape
    q_dev = rows_n * q_own
    chunks = x_all.shape[0]
    tall = BLOCKS * q_own
    count = rows_n * cols_n
    dense = q_dev + q_dev // 2
    pair = 3 * LANES
    order = (4, 3, 5, 2, 6, 1, 7)
    far = (10, 6, 9, 11, 5, 7, 8, 2, 14, 13, 15, 12, 4, 3, 1)

    def row_at(k):
        return lax.rem(me_r + k, rows_n)

    barrier = pltpu.get_barrier_semaphore()
    def greet(**to):
        pl.semaphore_signal(barrier, inc=1, device_id=to, device_id_type=MESH)

    for k in order:
        greet(row=row_at(k))
    cp_p = pltpu.make_async_copy(panels, p_buf, local_sem.at[0])
    cp_o = pltpu.make_async_copy(owner, o_buf, local_sem.at[1])
    cp_t = pltpu.make_async_copy(amp, t_buf, local_sem.at[2])
    cp_w = pltpu.make_async_copy(coeff_t, w_buf, local_sem.at[3])
    cp_p.start()
    cp_o.start()
    cp_t.start()
    cp_w.start()

    @pl.when(summing)
    def _():
        for k in far:
            greet(col=lax.rem(me_c + k, cols_n))
        for k in far + (0,):
            greet(col=lax.rem(me_c + k, cols_n), aux=0)

    @pl.when(jnp.logical_not(summing))
    def _():
        for k in order + (0,):
            greet(row=row_at(k), aux=hub)

    x_stage[...] = jnp.zeros_like(x_stage)
    cp_p.wait()
    for t in range(chunks):
        for kb in range(BLOCKS):
            start = (t * BLOCKS + kb) * WIDTH
            width = min(WIDTH, depth - start)
            if width > 0:
                x_stage[t, pl.ds(kb * q_own, q_own), pl.ds(0, width)] = p_buf[
                    :, pl.ds(start, width)
                ].astype(F32)
    own_rows = pl.ds(pl.multiple_of(me_r * tall, tall), tall)
    for t in range(chunks):
        x_all[t, own_rows, :] = x_stage[t].astype(BF16)

    @pl.when(summing)
    def _():
        pl.semaphore_wait(barrier, 2 * rows_n - 1 + cols_n - 1)

    @pl.when(jnp.logical_not(summing))
    def _():
        pl.semaphore_wait(barrier, rows_n - 1 + cols_n)


    def panel_copy(t, source, to):
        rows = x_all.at[t, pl.ds(pl.multiple_of(source * tall, tall), tall), :]
        return pltpu.make_async_remote_copy(
            src_ref=rows,
            dst_ref=rows,
            send_sem=xs.at[t],
            recv_sem=xr.at[t],
            device_id={"row": to},
            device_id_type=MESH,
        )

    for t in range(chunks):
        for k in order:
            panel_copy(t, me_r, row_at(k)).start()

    names[...] = jnp.full_like(names, -1)
    cp_o.wait()
    names[:, pl.ds(0, nao)] = o_buf[...]
    tri = (iota((WIDTH, WIDTH), 0) < iota((WIDTH, WIDTH), 1)).astype(BF16)
    carry = jnp.zeros((count, 1), F32)
    for b in range(names.shape[1] // WIDTH):
        name = names[:, pl.ds(b * WIDTH, WIDTH)]
        ones = jnp.where(name == iota((count, WIDTH), 0), 1.0, 0.0).astype(F32)
        before = jnp.dot(ones.astype(BF16), tri, preferred_element_type=F32) + carry
        slot = jnp.sum(ones * before, axis=0, keepdims=True)
        carry = carry + jnp.sum(ones, axis=1, keepdims=True)
        at_row = lax.div(name, jnp.int32(cols_n))
        at_col = name - at_row * cols_n
        at_pair = lax.div(at_col, jnp.int32(2))
        odd = at_col - at_pair * 2
        base = (at_pair * pair + at_row * HEAD).astype(F32)
        early = base + (odd * LANES).astype(F32) + slot
        late = base + (odd * TAIL + (2 * LANES - HEAD)).astype(F32) + slot
        lane = jnp.where(slot < HEAD, early, late)
        lane = jnp.where(name < 0, -1.0, lane)
        place[pl.ds(b * WIDTH, WIDTH), :] = jnp.broadcast_to(lane, (LANES, WIDTH)).T

    @pl.loop(0, spread.shape[1] // LANES)
    def _(b):
        at = (iota((nao, LANES), 1) + b * LANES).astype(F32)
        hot = jnp.where(place[pl.ds(0, nao), :] == at, 1.0, 0.0)
        spread[:, pl.ds(pl.multiple_of(b * LANES, LANES), LANES)] = hot.astype(BF16)

    for i in range(rows_n):
        a = iota((LANES, rows_n * q_dev), 0)
        n = iota((LANES, rows_n * q_dev), 1)
        head = jnp.where((a < q_dev) & (n == a * rows_n + i), 1.0, 0.0)
        tail = jnp.where(
            (a >= q_dev) & (a < dense) & (lax.rem(n, LANES) == (a - q_dev) * rows_n + i), 1.0, 0.0
        )
        expand[pl.ds(i * LANES, LANES), :] = jnp.concatenate([head, tail], axis=1).astype(BF16)

    cp_t.wait()
    partial = jnp.zeros((q_dev, virt), F32)
    for t in range(chunks):
        others = x_all.at[t, pl.ds(0, (rows_n - 1) * tall), :]
        pltpu.make_async_copy(others, others, xr.at[t]).wait()
        for kb in range(BLOCKS):
            start = (t * BLOCKS + kb) * WIDTH
            width = min(WIDTH, depth - start)
            if width <= 0:
                continue
            q = iota((q_dev, LANES), 0)
            source = lax.div(q, q_own) * tall + kb * q_own + lax.rem(q, q_own)
            pick = jnp.where(source == iota((q_dev, LANES), 1), 1.0, 0.0).astype(BF16)
            g = jnp.dot(pick, x_all[t], preferred_element_type=F32).astype(BF16)
            partial = partial + lax.dot_general(
                g[:, :width], t_buf[:, pl.ds(start, width)], NT, preferred_element_type=F32
            )

    cp_w.wait()
    half = jnp.dot(split(partial), w_buf[...], preferred_element_type=F32)
    half = split(half[:q_dev] + half[q_dev:])

    def partial_copy(aux, source, to):
        return pltpu.make_async_remote_copy(
            src_ref=d_buf.at[to],
            dst_ref=r_buf.at[aux, source],
            send_sem=ds.at[0],
            recv_sem=dr.at[aux],
            device_id={"col": to, "aux": hub},
            device_id_type=MESH,
        )

    quads = cols_n // QUAD
    my_quad = lax.div(me_c, QUAD)
    lower = lax.rem(iota((q_dev // 2, LANES), 1), 2 * TAIL) < TAIL
    for step in range(quads):
        quad = lax.rem(my_quad + (2, 1, 3, 0)[step], quads)
        lanes = QUAD // 2 * pair
        part = spread[:, pl.ds(pl.multiple_of(quad * lanes, lanes), lanes)]
        slots = jnp.dot(half, part, preferred_element_type=F32)
        slots = slots[:q_dev] + slots[q_dev:]
        for j in range(QUAD):
            to = quad * QUAD + j
            first = j // 2 * pair
            head = slots[:, first + j % 2 * LANES : first + (j % 2 + 1) * LANES]
            tail = slots[:, first + 2 * LANES : first + 3 * LANES]
            upper_q, lower_q = tail[: q_dev // 2], tail[q_dev // 2 :]
            if j % 2:
                upper_q = pltpu.roll(upper_q, LANES - TAIL, 1)
            else:
                lower_q = pltpu.roll(lower_q, TAIL, 1)
            d_buf[to, pl.ds(0, q_dev), :] = head
            d_buf[to, pl.ds(q_dev, q_dev // 2), :] = jnp.where(lower, upper_q, lower_q)
        for k in (2, 1, 3, 0):
            to = quad * QUAD + lax.rem(me_c + k, QUAD)
            if step < quads - 1 or k:
                partial_copy(me_a, me_c, to).start()
            else:

                @pl.when(jnp.logical_not(summing))
                def _():
                    partial_copy(me_a, me_c, to).start()

    for t in range(chunks):
        sent = x_all.at[t, pl.ds(0, (rows_n - 1) * tall), :]
        pltpu.make_async_copy(sent, sent, xs.at[t]).wait()
    def slot_copy(aux, source, to):
        return pltpu.make_async_remote_copy(
            src_ref=z_buf.at[aux, pl.ds(pl.multiple_of(to * HEAD, HEAD), HEAD), :],
            dst_ref=z_all.at[pl.ds(pl.multiple_of(source * HEAD, HEAD), HEAD), :],
            send_sem=zs.at[aux],
            recv_sem=zr.at[0],
            device_id={"row": to, "aux": aux},
            device_id_type=MESH,
        )

    @pl.when(summing)
    def _():
        for aux in (hub,) + tuple(range(hub)):
            if aux == hub:
                others = r_buf.at[aux, pl.ds(0, cols_n - 1)]
                total = d_buf[me_c]
            else:
                others = r_buf.at[aux]
                total = jnp.zeros((dense, LANES), F32)
            pltpu.make_async_copy(others, others, dr.at[aux]).wait()
            for k in range(1 if aux == hub else 0, cols_n):
                total = total + r_buf[aux, lax.rem(me_c + k, cols_n)]
            total = jnp.concatenate([total, jnp.zeros((LANES - dense, LANES), F32)], axis=0)
            z_buf[aux] = total.T.astype(BF16)
            for k in order:
                slot_copy(aux, me_r, row_at(k)).start()
            if aux != hub:
                slot_copy(aux, me_r, me_r).start()
        own = pl.ds(pl.multiple_of(me_r * HEAD, HEAD), HEAD)
        z_all[own, :] = z_buf[hub, own, :]
        partials_sent = d_buf.at[pl.ds(0, cols_n - 1)]
        pltpu.make_async_copy(partials_sent, partials_sent, ds.at[0]).wait()
        others = z_all.at[pl.ds(0, (rows_n - 1) * HEAD), :]
        pltpu.make_async_copy(others, others, zr.at[0]).wait()

    @pl.when(jnp.logical_not(summing))
    def _():
        pltpu.make_async_copy(d_buf, d_buf, ds.at[0]).wait()
        pltpu.make_async_copy(z_all, z_all, zr.at[0]).wait()

    got = jnp.concatenate([z_all[pl.ds(i * HEAD, HEAD), :] for i in range(rows_n)], axis=1)
    result = jnp.dot(got, expand[...], preferred_element_type=F32)
    wide = rows_n * q_dev
    tail = jnp.concatenate(
        [result[:TAIL, wide : wide + LANES], result[TAIL:, wide + LANES :]], axis=1
    )
    out[...] = jnp.concatenate([result[:, :wide], tail], axis=0).astype(BF16)

    @pl.when(summing)
    def _():
        for aux in range(aux_n):
            parts = rows_n - 1 if aux == hub else rows_n
            slots_sent = z_buf.at[aux, pl.ds(0, parts * HEAD), :]
            pltpu.make_async_copy(slots_sent, slots_sent, zs.at[aux]).wait()


def shards(panels, amplitudes, virt_coeff, row_owner):
    rows_n = lax.axis_size("row")
    cols_n = lax.axis_size("col")
    aux_n = lax.axis_size("aux")
    q_own, depth = panels.shape
    nao, virt = virt_coeff.shape
    q_dev = rows_n * q_own
    chunks = -(-depth // (BLOCKS * WIDTH))
    tall = BLOCKS * q_own
    padded = -(-nao // WIDTH) * WIDTH
    dense = q_dev + q_dev // 2
    vmem = pltpu.VMEM
    dma = pltpu.SemaphoreType.DMA
    return pl.pallas_call(
        functools.partial(kernel, rows_n, cols_n, aux_n),
        out_shape=pltpu.VMEM((HEAD + TAIL, rows_n * q_dev), BF16),
        in_specs=[pl.BlockSpec(memory_space=pl.ANY)] * 4,
        out_specs=pl.BlockSpec(memory_space=pltpu.VMEM),
        scratch_shapes=[
            vmem(amplitudes.shape, BF16),
            vmem((virt, nao), BF16),
            vmem(panels.shape, BF16),
            vmem((1, nao), jnp.int32),
            vmem((1, padded), jnp.int32),
            vmem((chunks, tall, WIDTH), F32),
            vmem((chunks, rows_n * tall, WIDTH), BF16),
            vmem((padded, LANES), F32),
            vmem((nao, cols_n // 2 * 3 * LANES), BF16),
            vmem((rows_n * LANES, 2 * rows_n * q_dev), BF16),
            vmem((cols_n, dense, LANES), F32),
            vmem((aux_n, cols_n, dense, LANES), F32),
            vmem((aux_n, rows_n * HEAD, LANES), BF16),
            vmem((rows_n * HEAD, LANES), BF16),
            dma((4,)),
            dma((chunks,)),
            dma((chunks,)),
            dma((1,)),
            dma((aux_n,)),
            dma((aux_n,)),
            dma((1,)),
        ],
        compiler_params=pltpu.CompilerParams(
            collective_id=0, has_side_effects=True, vmem_limit_bytes=56 * 1024 * 1024
        ),
        cost_estimate=pl.CostEstimate(
            flops=2 * virt * depth * LANES, bytes_accessed=amplitudes.size * 2, transcendentals=0
        ),
        name="density",
    )(panels, row_owner.reshape(1, nao), amplitudes, virt_coeff.T)


def solution(mesh):
    placed = (P(("aux", "row"), "col"), P("row", "col"), P(), P())
    return jax.shard_map(
        shards, mesh=mesh, in_specs=placed, out_specs=P(("row", "col"), "aux"), check_vma=False
    )
```

```python
import functools
import jax
import jax.numpy as jnp
from jax import lax
from jax.experimental import pallas as pl
from jax.experimental.pallas import tpu as pltpu
from jax.sharding import PartitionSpec as P

F32 = jnp.float32
BF16 = jnp.bfloat16
MESH = pl.DeviceIdType.MESH

LANES = 128
BLOCKS = 4
WIDTH = 256
HEAD = 16
TAIL = 8
QUAD = 4


def split(x):
    hi = x.astype(BF16)
    lo = (x - hi.astype(F32)).astype(BF16)
    return jnp.concatenate([hi, lo], axis=0)


def iota(shape, dim):
    return lax.broadcasted_iota(jnp.int32, shape, dim)


def kernel(
    rows_n,
    cols_n,
    aux_n,
    panels,
    owner,
    amp,
    coeff_t,
    out,
    t_buf,
    tt_buf,
    w_buf,
    p_buf,
    o_buf,
    names,
    x_stage,
    x_all,
    place,
    spread,
    expand,
    d_buf,
    r_buf,
    z_buf,
    z_all,
    local_sem,
    xs,
    xr,
    ds,
    dr,
    zs,
    zr,
):
    me_r = lax.axis_index("row")
    me_c = lax.axis_index("col")
    me_a = lax.axis_index("aux")
    hub = aux_n - 1
    summing = me_a == hub
    q_own, depth = panels.shape
    virt, nao = coeff_t.shape
    q_dev = rows_n * q_own
    chunks = x_all.shape[0]
    tall = BLOCKS * q_own
    count = rows_n * cols_n
    dense = q_dev + q_dev // 2
    pair = 3 * LANES
    order = (4, 3, 5, 2, 6, 1, 7)
    far = (10, 6, 9, 11, 5, 7, 8, 2, 14, 13, 15, 12, 4, 3, 1)

    def row_at(k):
        return lax.rem(me_r + k, rows_n)

    barrier = pltpu.get_barrier_semaphore()
    def greet(**to):
        pl.semaphore_signal(barrier, inc=1, device_id=to, device_id_type=MESH)

    for k in order:
        greet(row=row_at(k))
    cp_p = pltpu.make_async_copy(panels, p_buf, local_sem.at[0])
    cp_o = pltpu.make_async_copy(owner, o_buf, local_sem.at[1])
    cp_t = pltpu.make_async_copy(amp, t_buf, local_sem.at[2])
    cp_w = pltpu.make_async_copy(coeff_t, w_buf, local_sem.at[3])
    cp_p.start()
    cp_o.start()
    cp_t.start()
    cp_w.start()

    @pl.when(summing)
    def _():
        for k in far:
            greet(col=lax.rem(me_c + k, cols_n))
        for k in far + (0,):
            greet(col=lax.rem(me_c + k, cols_n), aux=0)

    @pl.when(jnp.logical_not(summing))
    def _():
        for k in order + (0,):
            greet(row=row_at(k), aux=hub)

    def fill_slots():
        names[...] = jnp.full_like(names, -1)
        cp_o.wait()
        names[:, pl.ds(0, nao)] = o_buf[...]
        tri = (iota((WIDTH, WIDTH), 0) < iota((WIDTH, WIDTH), 1)).astype(BF16)
        carry = jnp.zeros((count, 1), F32)
        for b in range(names.shape[1] // WIDTH):
            name = names[:, pl.ds(b * WIDTH, WIDTH)]
            ones = jnp.where(name == iota((count, WIDTH), 0), 1.0, 0.0).astype(F32)
            before = jnp.dot(ones.astype(BF16), tri, preferred_element_type=F32) + carry
            slot = jnp.sum(ones * before, axis=0, keepdims=True)
            carry = carry + jnp.sum(ones, axis=1, keepdims=True)
            at_row = lax.div(name, jnp.int32(cols_n))
            at_col = name - at_row * cols_n
            at_pair = lax.div(at_col, jnp.int32(2))
            odd = at_col - at_pair * 2
            base = (at_pair * pair + at_row * HEAD).astype(F32)
            early = base + (odd * LANES).astype(F32) + slot
            late = base + (odd * TAIL + (2 * LANES - HEAD)).astype(F32) + slot
            lane = jnp.where(slot < HEAD, early, late)
            lane = jnp.where(name < 0, -1.0, lane)
            place[pl.ds(b * WIDTH, WIDTH), :] = jnp.broadcast_to(lane, (LANES, WIDTH)).T

        @pl.loop(0, spread.shape[1] // LANES)
        def _(b):
            at = (iota((nao, LANES), 1) + b * LANES).astype(F32)
            hot = jnp.where(place[pl.ds(0, nao), :] == at, 1.0, 0.0)
            spread[:, pl.ds(pl.multiple_of(b * LANES, LANES), LANES)] = hot.astype(BF16)

    x_stage[...] = jnp.zeros_like(x_stage)
    cp_p.wait()
    for t in range(chunks):
        for kb in range(BLOCKS):
            start = (t * BLOCKS + kb) * WIDTH
            width = min(WIDTH, depth - start)
            if width > 0:
                x_stage[t, pl.ds(kb * q_own, q_own), pl.ds(0, width)] = p_buf[
                    :, pl.ds(start, width)
                ].astype(F32)
    own_rows = pl.ds(pl.multiple_of(me_r * tall, tall), tall)
    for t in range(chunks):
        x_all[t, own_rows, :] = x_stage[t].astype(BF16)

    early = me_r < rows_n // 2

    @pl.when(early)
    def _():
        fill_slots()

    @pl.when(summing)
    def _():
        pl.semaphore_wait(barrier, 2 * rows_n - 1 + cols_n - 1)

    @pl.when(jnp.logical_not(summing))
    def _():
        pl.semaphore_wait(barrier, rows_n - 1 + cols_n)


    def panel_copy(t, source, to):
        rows = x_all.at[t, pl.ds(pl.multiple_of(source * tall, tall), tall), :]
        return pltpu.make_async_remote_copy(
            src_ref=rows,
            dst_ref=rows,
            send_sem=xs.at[t],
            recv_sem=xr.at[t],
            device_id={"row": to},
            device_id_type=MESH,
        )

    for t in range(chunks):
        for k in order:
            panel_copy(t, me_r, row_at(k)).start()

    @pl.when(jnp.logical_not(early))
    def _():
        fill_slots()

    for i in range(rows_n):
        a = iota((LANES, rows_n * q_dev), 0)
        n = iota((LANES, rows_n * q_dev), 1)
        head = jnp.where((a < q_dev) & (n == a * rows_n + i), 1.0, 0.0)
        tail = jnp.where(
            (a >= q_dev) & (a < dense) & (lax.rem(n, LANES) == (a - q_dev) * rows_n + i), 1.0, 0.0
        )
        expand[pl.ds(i * LANES, LANES), :] = jnp.concatenate([head, tail], axis=1).astype(BF16)

    cp_t.wait()
    for k in range(0, depth, WIDTH):
        width = min(WIDTH, depth - k)
        tt_buf[pl.ds(k, width), :] = t_buf[:, pl.ds(k, width)].T

    partial = jnp.zeros((q_dev, virt), F32)
    for t in range(chunks):
        others = x_all.at[t, pl.ds(0, (rows_n - 1) * tall), :]
        pltpu.make_async_copy(others, others, xr.at[t]).wait()
        for kb in range(BLOCKS):
            start = (t * BLOCKS + kb) * WIDTH
            width = min(WIDTH, depth - start)
            if width <= 0:
                continue
            q = iota((q_dev, LANES), 0)
            source = lax.div(q, q_own) * tall + kb * q_own + lax.rem(q, q_own)
            pick = jnp.where(source == iota((q_dev, LANES), 1), 1.0, 0.0).astype(BF16)
            g = jnp.dot(pick, x_all[t], preferred_element_type=F32).astype(BF16)
            partial = partial + jnp.dot(
                g[:, :width], tt_buf[pl.ds(start, width), :], preferred_element_type=F32
            )

    cp_w.wait()
    half = jnp.dot(split(partial), w_buf[...], preferred_element_type=F32)
    half = split(half[:q_dev] + half[q_dev:])

    def partial_copy(aux, source, to):
        return pltpu.make_async_remote_copy(
            src_ref=d_buf.at[to],
            dst_ref=r_buf.at[aux, source],
            send_sem=ds.at[0],
            recv_sem=dr.at[aux],
            device_id={"col": to, "aux": hub},
            device_id_type=MESH,
        )

    quads = cols_n // QUAD
    my_quad = lax.div(me_c, QUAD)
    lower = lax.rem(iota((q_dev // 2, LANES), 1), 2 * TAIL) < TAIL
    for step in range(quads):
        quad = lax.rem(my_quad + (2, 1, 3, 0)[step], quads)
        lanes = QUAD // 2 * pair
        part = spread[:, pl.ds(pl.multiple_of(quad * lanes, lanes), lanes)]
        slots = jnp.dot(half, part, preferred_element_type=F32)
        slots = slots[:q_dev] + slots[q_dev:]
        for j in range(QUAD):
            to = quad * QUAD + j
            first = j // 2 * pair
            head = slots[:, first + j % 2 * LANES : first + (j % 2 + 1) * LANES]
            tail = slots[:, first + 2 * LANES : first + 3 * LANES]
            upper_q, lower_q = tail[: q_dev // 2], tail[q_dev // 2 :]
            if j % 2:
                upper_q = pltpu.roll(upper_q, LANES - TAIL, 1)
            else:
                lower_q = pltpu.roll(lower_q, TAIL, 1)
            d_buf[to, pl.ds(0, q_dev), :] = head
            d_buf[to, pl.ds(q_dev, q_dev // 2), :] = jnp.where(lower, upper_q, lower_q)
        for k in (2, 1, 3, 0):
            to = quad * QUAD + lax.rem(me_c + k, QUAD)
            if step < quads - 1 or k:
                partial_copy(me_a, me_c, to).start()
            else:

                @pl.when(jnp.logical_not(summing))
                def _():
                    partial_copy(me_a, me_c, to).start()

    for t in range(chunks):
        sent = x_all.at[t, pl.ds(0, (rows_n - 1) * tall), :]
        pltpu.make_async_copy(sent, sent, xs.at[t]).wait()
    def slot_copy(aux, source, to):
        return pltpu.make_async_remote_copy(
            src_ref=z_buf.at[aux, pl.ds(pl.multiple_of(to * HEAD, HEAD), HEAD), :],
            dst_ref=z_all.at[pl.ds(pl.multiple_of(source * HEAD, HEAD), HEAD), :],
            send_sem=zs.at[aux],
            recv_sem=zr.at[0],
            device_id={"row": to, "aux": aux},
            device_id_type=MESH,
        )

    @pl.when(summing)
    def _():
        for aux in (hub,) + tuple(range(hub)):
            if aux == hub:
                others = r_buf.at[aux, pl.ds(0, cols_n - 1)]
                total = d_buf[me_c]
            else:
                others = r_buf.at[aux]
                total = jnp.zeros((dense, LANES), F32)
            pltpu.make_async_copy(others, others, dr.at[aux]).wait()
            for k in range(1 if aux == hub else 0, cols_n):
                total = total + r_buf[aux, lax.rem(me_c + k, cols_n)]
            total = jnp.concatenate([total, jnp.zeros((LANES - dense, LANES), F32)], axis=0)
            z_buf[aux] = total.T.astype(BF16)
            for k in order:
                slot_copy(aux, me_r, row_at(k)).start()
            if aux != hub:
                slot_copy(aux, me_r, me_r).start()
        own = pl.ds(pl.multiple_of(me_r * HEAD, HEAD), HEAD)
        z_all[own, :] = z_buf[hub, own, :]
        partials_sent = d_buf.at[pl.ds(0, cols_n - 1)]
        pltpu.make_async_copy(partials_sent, partials_sent, ds.at[0]).wait()
        others = z_all.at[pl.ds(0, (rows_n - 1) * HEAD), :]
        pltpu.make_async_copy(others, others, zr.at[0]).wait()

    @pl.when(jnp.logical_not(summing))
    def _():
        pltpu.make_async_copy(d_buf, d_buf, ds.at[0]).wait()
        pltpu.make_async_copy(z_all, z_all, zr.at[0]).wait()

    got = jnp.concatenate([z_all[pl.ds(i * HEAD, HEAD), :] for i in range(rows_n)], axis=1)
    result = jnp.dot(got, expand[...], preferred_element_type=F32)
    wide = rows_n * q_dev
    tail = jnp.concatenate(
        [result[:TAIL, wide : wide + LANES], result[TAIL:, wide + LANES :]], axis=1
    )
    out[...] = jnp.concatenate([result[:, :wide], tail], axis=0).astype(BF16)

    @pl.when(summing)
    def _():
        for aux in range(aux_n):
            parts = rows_n - 1 if aux == hub else rows_n
            slots_sent = z_buf.at[aux, pl.ds(0, parts * HEAD), :]
            pltpu.make_async_copy(slots_sent, slots_sent, zs.at[aux]).wait()


def shards(panels, amplitudes, virt_coeff, row_owner):
    rows_n = lax.axis_size("row")
    cols_n = lax.axis_size("col")
    aux_n = lax.axis_size("aux")
    q_own, depth = panels.shape
    nao, virt = virt_coeff.shape
    q_dev = rows_n * q_own
    chunks = -(-depth // (BLOCKS * WIDTH))
    tall = BLOCKS * q_own
    padded = -(-nao // WIDTH) * WIDTH
    dense = q_dev + q_dev // 2
    vmem = pltpu.VMEM
    dma = pltpu.SemaphoreType.DMA
    return pl.pallas_call(
        functools.partial(kernel, rows_n, cols_n, aux_n),
        out_shape=pltpu.VMEM((HEAD + TAIL, rows_n * q_dev), BF16),
        in_specs=[pl.BlockSpec(memory_space=pl.ANY)] * 4,
        out_specs=pl.BlockSpec(memory_space=pltpu.VMEM),
        scratch_shapes=[
            vmem(amplitudes.shape, BF16),
            vmem((depth, virt), BF16),
            vmem((virt, nao), BF16),
            vmem(panels.shape, BF16),
            vmem((1, nao), jnp.int32),
            vmem((1, padded), jnp.int32),
            vmem((chunks, tall, WIDTH), F32),
            vmem((chunks, rows_n * tall, WIDTH), BF16),
            vmem((padded, LANES), F32),
            vmem((nao, cols_n // 2 * 3 * LANES), BF16),
            vmem((rows_n * LANES, 2 * rows_n * q_dev), BF16),
            vmem((cols_n, dense, LANES), F32),
            vmem((aux_n, cols_n, dense, LANES), F32),
            vmem((aux_n, rows_n * HEAD, LANES), BF16),
            vmem((rows_n * HEAD, LANES), BF16),
            dma((4,)),
            dma((chunks,)),
            dma((chunks,)),
            dma((1,)),
            dma((aux_n,)),
            dma((aux_n,)),
            dma((1,)),
        ],
        compiler_params=pltpu.CompilerParams(
            collective_id=0, has_side_effects=True, vmem_limit_bytes=56 * 1024 * 1024
        ),
        cost_estimate=pl.CostEstimate(
            flops=2 * virt * depth * LANES, bytes_accessed=amplitudes.size * 2, transcendentals=0
        ),
        name="density",
    )(panels, row_owner.reshape(1, nao), amplitudes, virt_coeff.T)


def solution(mesh):
    placed = (P(("aux", "row"), "col"), P("row", "col"), P(), P())
    return jax.shard_map(
        shards, mesh=mesh, in_specs=placed, out_specs=P(("row", "col"), "aux"), check_vma=False
    )
```

```python
import functools
import jax
import jax.numpy as jnp
from jax import lax
from jax.experimental import pallas as pl
from jax.experimental.pallas import tpu as pltpu
from jax.sharding import PartitionSpec as P

F32 = jnp.float32
BF16 = jnp.bfloat16
MESH = pl.DeviceIdType.MESH
NT = (((1,), (1,)), ((), ()))

LANES = 128
BLOCKS = 4
WIDTH = 256
HEAD = 16
TAIL = 8
QUAD = 4


def split(x):
    hi = x.astype(BF16)
    lo = (x - hi.astype(F32)).astype(BF16)
    return jnp.concatenate([hi, lo], axis=0)


def iota(shape, dim):
    return lax.broadcasted_iota(jnp.int32, shape, dim)


def kernel(
    rows_n,
    cols_n,
    aux_n,
    panels,
    owner,
    amp,
    coeff_t,
    out,
    t_buf,
    w_buf,
    p_buf,
    o_buf,
    names,
    x_stage,
    x_all,
    place,
    spread,
    expand,
    d_buf,
    r_buf,
    z_buf,
    z_all,
    local_sem,
    xs,
    xr,
    ds,
    dr,
    zs,
    zr,
):
    me_r = lax.axis_index("row")
    me_c = lax.axis_index("col")
    me_a = lax.axis_index("aux")
    hub = aux_n - 1
    summing = me_a == hub
    q_own, depth = panels.shape
    virt, nao = coeff_t.shape
    q_dev = rows_n * q_own
    chunks = x_all.shape[0]
    tall = BLOCKS * q_own
    count = rows_n * cols_n
    dense = q_dev + q_dev // 2
    pair = 3 * LANES
    order = (4, 3, 5, 2, 6, 1, 7)
    far = (10, 6, 9, 11, 5, 7, 8, 2, 14, 13, 15, 12, 4, 3, 1)

    def row_at(k):
        return lax.rem(me_r + k, rows_n)

    barrier = pltpu.get_barrier_semaphore()
    def greet(**to):
        pl.semaphore_signal(barrier, inc=1, device_id=to, device_id_type=MESH)

    for k in order:
        greet(row=row_at(k))
    cp_p = pltpu.make_async_copy(panels, p_buf, local_sem.at[0])
    cp_o = pltpu.make_async_copy(owner, o_buf, local_sem.at[1])
    cp_t = pltpu.make_async_copy(amp, t_buf, local_sem.at[2])
    cp_w = pltpu.make_async_copy(coeff_t, w_buf, local_sem.at[3])
    cp_p.start()
    cp_o.start()
    cp_t.start()
    cp_w.start()

    @pl.when(summing)
    def _():
        for k in far:
            greet(col=lax.rem(me_c + k, cols_n))
        for k in far + (0,):
            greet(col=lax.rem(me_c + k, cols_n), aux=0)

    @pl.when(jnp.logical_not(summing))
    def _():
        for k in order + (0,):
            greet(row=row_at(k), aux=hub)

    x_stage[...] = jnp.zeros_like(x_stage)
    cp_p.wait()
    for t in range(chunks):
        for kb in range(BLOCKS):
            start = (t * BLOCKS + kb) * WIDTH
            width = min(WIDTH, depth - start)
            if width > 0:
                x_stage[t, pl.ds(kb * q_own, q_own), pl.ds(0, width)] = p_buf[
                    :, pl.ds(start, width)
                ].astype(F32)
    own_rows = pl.ds(pl.multiple_of(me_r * tall, tall), tall)
    for t in range(chunks):
        x_all[t, own_rows, :] = x_stage[t].astype(BF16)

    @pl.when(summing)
    def _():
        pl.semaphore_wait(barrier, 2 * rows_n - 1 + cols_n - 1)

    @pl.when(jnp.logical_not(summing))
    def _():
        pl.semaphore_wait(barrier, rows_n - 1 + cols_n)


    groups = ((0, 1), (1, chunks - 1))

    def panel_copy(g, source, to):
        rows = x_all.at[
            pl.ds(*groups[g]), pl.ds(pl.multiple_of(source * tall, tall), tall), :
        ]
        return pltpu.make_async_remote_copy(
            src_ref=rows,
            dst_ref=rows,
            send_sem=xs.at[g],
            recv_sem=xr.at[g],
            device_id={"row": to},
            device_id_type=MESH,
        )

    for g in range(len(groups)):
        for k in order:
            panel_copy(g, me_r, row_at(k)).start()

    names[...] = jnp.full_like(names, -1)
    cp_o.wait()
    names[:, pl.ds(0, nao)] = o_buf[...]
    tri = (iota((WIDTH, WIDTH), 0) < iota((WIDTH, WIDTH), 1)).astype(BF16)
    carry = jnp.zeros((count, 1), F32)
    for b in range(names.shape[1] // WIDTH):
        name = names[:, pl.ds(b * WIDTH, WIDTH)]
        ones = jnp.where(name == iota((count, WIDTH), 0), 1.0, 0.0).astype(F32)
        before = jnp.dot(ones.astype(BF16), tri, preferred_element_type=F32) + carry
        slot = jnp.sum(ones * before, axis=0, keepdims=True)
        carry = carry + jnp.sum(ones, axis=1, keepdims=True)
        at_row = lax.div(name, jnp.int32(cols_n))
        at_col = name - at_row * cols_n
        at_pair = lax.div(at_col, jnp.int32(2))
        odd = at_col - at_pair * 2
        base = (at_pair * pair + at_row * HEAD).astype(F32)
        early = base + (odd * LANES).astype(F32) + slot
        late = base + (odd * TAIL + (2 * LANES - HEAD)).astype(F32) + slot
        lane = jnp.where(slot < HEAD, early, late)
        lane = jnp.where(name < 0, -1.0, lane)
        place[pl.ds(b * WIDTH, WIDTH), :] = jnp.broadcast_to(lane, (LANES, WIDTH)).T

    @pl.loop(0, spread.shape[1] // LANES)
    def _(b):
        at = (iota((nao, LANES), 1) + b * LANES).astype(F32)
        hot = jnp.where(place[pl.ds(0, nao), :] == at, 1.0, 0.0)
        spread[:, pl.ds(pl.multiple_of(b * LANES, LANES), LANES)] = hot.astype(BF16)

    for i in range(rows_n):
        a = iota((LANES, rows_n * q_dev), 0)
        n = iota((LANES, rows_n * q_dev), 1)
        head = jnp.where((a < q_dev) & (n == a * rows_n + i), 1.0, 0.0)
        tail = jnp.where(
            (a >= q_dev) & (a < dense) & (lax.rem(n, LANES) == (a - q_dev) * rows_n + i), 1.0, 0.0
        )
        expand[pl.ds(i * LANES, LANES), :] = jnp.concatenate([head, tail], axis=1).astype(BF16)

    cp_t.wait()
    partial = jnp.zeros((q_dev, virt), F32)
    for t in range(chunks):
        for g, (first, size) in enumerate(groups):
            if t == first:
                others = x_all.at[pl.ds(first, size), pl.ds(0, (rows_n - 1) * tall), :]
                pltpu.make_async_copy(others, others, xr.at[g]).wait()
        for kb in range(BLOCKS):
            start = (t * BLOCKS + kb) * WIDTH
            width = min(WIDTH, depth - start)
            if width <= 0:
                continue
            q = iota((q_dev, LANES), 0)
            source = lax.div(q, q_own) * tall + kb * q_own + lax.rem(q, q_own)
            pick = jnp.where(source == iota((q_dev, LANES), 1), 1.0, 0.0).astype(BF16)
            part = jnp.dot(pick, x_all[t], preferred_element_type=F32).astype(BF16)
            partial = partial + lax.dot_general(
                part[:, :width], t_buf[:, pl.ds(start, width)], NT, preferred_element_type=F32
            )

    cp_w.wait()
    half = jnp.dot(split(partial), w_buf[...], preferred_element_type=F32)
    half = split(half[:q_dev] + half[q_dev:])

    def partial_copy(aux, source, to):
        return pltpu.make_async_remote_copy(
            src_ref=d_buf.at[to],
            dst_ref=r_buf.at[aux, source],
            send_sem=ds.at[0],
            recv_sem=dr.at[aux],
            device_id={"col": to, "aux": hub},
            device_id_type=MESH,
        )

    quads = cols_n // QUAD
    my_quad = lax.div(me_c, QUAD)
    lower = lax.rem(iota((q_dev // 2, LANES), 1), 2 * TAIL) < TAIL
    for step in range(quads):
        quad = lax.rem(my_quad + (2, 1, 3, 0)[step], quads)
        lanes = QUAD // 2 * pair
        part = spread[:, pl.ds(pl.multiple_of(quad * lanes, lanes), lanes)]
        slots = jnp.dot(half, part, preferred_element_type=F32)
        slots = slots[:q_dev] + slots[q_dev:]
        for j in range(QUAD):
            to = quad * QUAD + j
            first = j // 2 * pair
            head = slots[:, first + j % 2 * LANES : first + (j % 2 + 1) * LANES]
            tail = slots[:, first + 2 * LANES : first + 3 * LANES]
            upper_q, lower_q = tail[: q_dev // 2], tail[q_dev // 2 :]
            if j % 2:
                upper_q = pltpu.roll(upper_q, LANES - TAIL, 1)
            else:
                lower_q = pltpu.roll(lower_q, TAIL, 1)
            d_buf[to, pl.ds(0, q_dev), :] = head
            d_buf[to, pl.ds(q_dev, q_dev // 2), :] = jnp.where(lower, upper_q, lower_q)
        for k in (2, 1, 3, 0):
            to = quad * QUAD + lax.rem(me_c + k, QUAD)
            if step < quads - 1 or k:
                partial_copy(me_a, me_c, to).start()
            else:

                @pl.when(jnp.logical_not(summing))
                def _():
                    partial_copy(me_a, me_c, to).start()

    for g in range(len(groups)):
        sent = x_all.at[pl.ds(*groups[g]), pl.ds(0, (rows_n - 1) * tall), :]
        pltpu.make_async_copy(sent, sent, xs.at[g]).wait()
    def slot_copy(aux, source, to):
        return pltpu.make_async_remote_copy(
            src_ref=z_buf.at[aux, pl.ds(pl.multiple_of(to * HEAD, HEAD), HEAD), :],
            dst_ref=z_all.at[pl.ds(pl.multiple_of(source * HEAD, HEAD), HEAD), :],
            send_sem=zs.at[aux],
            recv_sem=zr.at[0],
            device_id={"row": to, "aux": aux},
            device_id_type=MESH,
        )

    @pl.when(summing)
    def _():
        for aux in (hub,) + tuple(range(hub)):
            if aux == hub:
                others = r_buf.at[aux, pl.ds(0, cols_n - 1)]
                total = d_buf[me_c]
            else:
                others = r_buf.at[aux]
                total = jnp.zeros((dense, LANES), F32)
            pltpu.make_async_copy(others, others, dr.at[aux]).wait()
            for k in range(1 if aux == hub else 0, cols_n):
                total = total + r_buf[aux, lax.rem(me_c + k, cols_n)]
            total = jnp.concatenate([total, jnp.zeros((LANES - dense, LANES), F32)], axis=0)
            z_buf[aux] = total.T.astype(BF16)
            for k in order:
                slot_copy(aux, me_r, row_at(k)).start()
            if aux != hub:
                slot_copy(aux, me_r, me_r).start()
        own = pl.ds(pl.multiple_of(me_r * HEAD, HEAD), HEAD)
        z_all[own, :] = z_buf[hub, own, :]
        partials_sent = d_buf.at[pl.ds(0, cols_n - 1)]
        pltpu.make_async_copy(partials_sent, partials_sent, ds.at[0]).wait()
        others = z_all.at[pl.ds(0, (rows_n - 1) * HEAD), :]
        pltpu.make_async_copy(others, others, zr.at[0]).wait()

    @pl.when(jnp.logical_not(summing))
    def _():
        pltpu.make_async_copy(d_buf, d_buf, ds.at[0]).wait()
        pltpu.make_async_copy(z_all, z_all, zr.at[0]).wait()

    got = jnp.concatenate([z_all[pl.ds(i * HEAD, HEAD), :] for i in range(rows_n)], axis=1)
    result = jnp.dot(got, expand[...], preferred_element_type=F32)
    wide = rows_n * q_dev
    tail = jnp.concatenate(
        [result[:TAIL, wide : wide + LANES], result[TAIL:, wide + LANES :]], axis=1
    )
    out[...] = jnp.concatenate([result[:, :wide], tail], axis=0).astype(BF16)

    @pl.when(summing)
    def _():
        for aux in range(aux_n):
            parts = rows_n - 1 if aux == hub else rows_n
            slots_sent = z_buf.at[aux, pl.ds(0, parts * HEAD), :]
            pltpu.make_async_copy(slots_sent, slots_sent, zs.at[aux]).wait()


def shards(panels, amplitudes, virt_coeff, row_owner):
    rows_n = lax.axis_size("row")
    cols_n = lax.axis_size("col")
    aux_n = lax.axis_size("aux")
    q_own, depth = panels.shape
    nao, virt = virt_coeff.shape
    q_dev = rows_n * q_own
    chunks = -(-depth // (BLOCKS * WIDTH))
    tall = BLOCKS * q_own
    padded = -(-nao // WIDTH) * WIDTH
    dense = q_dev + q_dev // 2
    vmem = pltpu.VMEM
    dma = pltpu.SemaphoreType.DMA
    return pl.pallas_call(
        functools.partial(kernel, rows_n, cols_n, aux_n),
        out_shape=pltpu.VMEM((HEAD + TAIL, rows_n * q_dev), BF16),
        in_specs=[pl.BlockSpec(memory_space=pl.ANY)] * 4,
        out_specs=pl.BlockSpec(memory_space=pltpu.VMEM),
        scratch_shapes=[
            vmem(amplitudes.shape, BF16),
            vmem((virt, nao), BF16),
            vmem(panels.shape, BF16),
            vmem((1, nao), jnp.int32),
            vmem((1, padded), jnp.int32),
            vmem((chunks, tall, WIDTH), F32),
            vmem((chunks, rows_n * tall, WIDTH), BF16),
            vmem((padded, LANES), F32),
            vmem((nao, cols_n // 2 * 3 * LANES), BF16),
            vmem((rows_n * LANES, 2 * rows_n * q_dev), BF16),
            vmem((cols_n, dense, LANES), F32),
            vmem((aux_n, cols_n, dense, LANES), F32),
            vmem((aux_n, rows_n * HEAD, LANES), BF16),
            vmem((rows_n * HEAD, LANES), BF16),
            dma((4,)),
            dma((chunks,)),
            dma((chunks,)),
            dma((1,)),
            dma((aux_n,)),
            dma((aux_n,)),
            dma((1,)),
        ],
        compiler_params=pltpu.CompilerParams(
            collective_id=0, has_side_effects=True, vmem_limit_bytes=56 * 1024 * 1024
        ),
        cost_estimate=pl.CostEstimate(
            flops=2 * virt * depth * LANES, bytes_accessed=amplitudes.size * 2, transcendentals=0
        ),
        name="density",
    )(panels, row_owner.reshape(1, nao), amplitudes, virt_coeff.T)


def solution(mesh):
    placed = (P(("aux", "row"), "col"), P("row", "col"), P(), P())
    return jax.shard_map(
        shards, mesh=mesh, in_specs=placed, out_specs=P(("row", "col"), "aux"), check_vma=False
    )
```

```python
import functools
import jax
import jax.numpy as jnp
from jax import lax
from jax.experimental import pallas as pl
from jax.experimental.pallas import tpu as pltpu
from jax.sharding import PartitionSpec as P

F32 = jnp.float32
BF16 = jnp.bfloat16
MESH = pl.DeviceIdType.MESH
NT = (((1,), (1,)), ((), ()))

LANES = 128
BLOCKS = 4
WIDTH = 256
HEAD = 16
TAIL = 8
QUAD = 4


def split(x):
    hi = x.astype(BF16)
    lo = (x - hi.astype(F32)).astype(BF16)
    return jnp.concatenate([hi, lo], axis=0)


def iota(shape, dim):
    return lax.broadcasted_iota(jnp.int32, shape, dim)


def kernel(
    rows_n,
    cols_n,
    aux_n,
    panels,
    owner,
    amp,
    coeff_t,
    out,
    t_buf,
    w_buf,
    p_buf,
    o_buf,
    names,
    x_stage,
    x_all,
    place,
    spread,
    expand,
    d_buf,
    r_buf,
    z_buf,
    z_all,
    local_sem,
    xs,
    xr,
    ds,
    dr,
    zs,
    zr,
):
    me_r = lax.axis_index("row")
    me_c = lax.axis_index("col")
    me_a = lax.axis_index("aux")
    hub = aux_n - 1
    summing = me_a == hub
    q_own, depth = panels.shape
    virt, nao = coeff_t.shape
    q_dev = rows_n * q_own
    chunks = x_all.shape[0]
    tall = BLOCKS * q_own
    count = rows_n * cols_n
    dense = q_dev + q_dev // 2
    pair = 3 * LANES
    order = (4, 3, 5, 2, 6, 1, 7)
    far = (10, 6, 9, 11, 5, 7, 8, 2, 14, 13, 15, 12, 4, 3, 1)

    def row_at(k):
        return lax.rem(me_r + k, rows_n)

    barrier = pltpu.get_barrier_semaphore()
    def greet(**to):
        pl.semaphore_signal(barrier, inc=1, device_id=to, device_id_type=MESH)

    for k in order:
        greet(row=row_at(k))
    cp_p = pltpu.make_async_copy(panels, p_buf, local_sem.at[0])
    cp_o = pltpu.make_async_copy(owner, o_buf, local_sem.at[1])
    cp_t = pltpu.make_async_copy(amp, t_buf, local_sem.at[2])
    cp_w = pltpu.make_async_copy(coeff_t, w_buf, local_sem.at[3])
    cp_p.start()
    cp_o.start()
    cp_t.start()
    cp_w.start()

    @pl.when(summing)
    def _():
        for k in far:
            greet(col=lax.rem(me_c + k, cols_n))
        for k in far + (0,):
            greet(col=lax.rem(me_c + k, cols_n), aux=0)

    @pl.when(jnp.logical_not(summing))
    def _():
        for k in order + (0,):
            greet(row=row_at(k), aux=hub)

    def fill_slots():
        names[...] = jnp.full_like(names, -1)
        cp_o.wait()
        names[:, pl.ds(0, nao)] = o_buf[...]
        tri = (iota((WIDTH, WIDTH), 0) < iota((WIDTH, WIDTH), 1)).astype(BF16)
        carry = jnp.zeros((count, 1), F32)
        for b in range(names.shape[1] // WIDTH):
            name = names[:, pl.ds(b * WIDTH, WIDTH)]
            ones = jnp.where(name == iota((count, WIDTH), 0), 1.0, 0.0).astype(F32)
            before = jnp.dot(ones.astype(BF16), tri, preferred_element_type=F32) + carry
            slot = jnp.sum(ones * before, axis=0, keepdims=True)
            carry = carry + jnp.sum(ones, axis=1, keepdims=True)
            at_row = lax.div(name, jnp.int32(cols_n))
            at_col = name - at_row * cols_n
            at_pair = lax.div(at_col, jnp.int32(2))
            odd = at_col - at_pair * 2
            base = (at_pair * pair + at_row * HEAD).astype(F32)
            early = base + (odd * LANES).astype(F32) + slot
            late = base + (odd * TAIL + (2 * LANES - HEAD)).astype(F32) + slot
            lane = jnp.where(slot < HEAD, early, late)
            lane = jnp.where(name < 0, -1.0, lane)
            place[pl.ds(b * WIDTH, WIDTH), :] = jnp.broadcast_to(lane, (LANES, WIDTH)).T

        @pl.loop(0, spread.shape[1] // LANES)
        def _(b):
            at = (iota((nao, LANES), 1) + b * LANES).astype(F32)
            hot = jnp.where(place[pl.ds(0, nao), :] == at, 1.0, 0.0)
            spread[:, pl.ds(pl.multiple_of(b * LANES, LANES), LANES)] = hot.astype(BF16)

    x_stage[...] = jnp.zeros_like(x_stage)
    cp_p.wait()
    for t in range(chunks):
        for kb in range(BLOCKS):
            start = (t * BLOCKS + kb) * WIDTH
            width = min(WIDTH, depth - start)
            if width > 0:
                x_stage[t, pl.ds(kb * q_own, q_own), pl.ds(0, width)] = p_buf[
                    :, pl.ds(start, width)
                ].astype(F32)
    own_rows = pl.ds(pl.multiple_of(me_r * tall, tall), tall)
    for t in range(chunks):
        x_all[t, own_rows, :] = x_stage[t].astype(BF16)

    early = me_r < rows_n // 2

    @pl.when(early)
    def _():
        fill_slots()

    @pl.when(summing)
    def _():
        pl.semaphore_wait(barrier, 2 * rows_n - 1 + cols_n - 1)

    @pl.when(jnp.logical_not(summing))
    def _():
        pl.semaphore_wait(barrier, rows_n - 1 + cols_n)


    def panel_copy(t, source, to):
        rows = x_all.at[t, pl.ds(pl.multiple_of(source * tall, tall), tall), :]
        return pltpu.make_async_remote_copy(
            src_ref=rows,
            dst_ref=rows,
            send_sem=xs.at[t],
            recv_sem=xr.at[t],
            device_id={"row": to},
            device_id_type=MESH,
        )

    for t in range(chunks):
        for k in order:
            panel_copy(t, me_r, row_at(k)).start()

    @pl.when(jnp.logical_not(early))
    def _():
        fill_slots()

    for i in range(rows_n):
        a = iota((LANES, rows_n * q_dev), 0)
        n = iota((LANES, rows_n * q_dev), 1)
        head = jnp.where((a < q_dev) & (n == a * rows_n + i), 1.0, 0.0)
        tail = jnp.where(
            (a >= q_dev) & (a < dense) & (lax.rem(n, LANES) == (a - q_dev) * rows_n + i), 1.0, 0.0
        )
        expand[pl.ds(i * LANES, LANES), :] = jnp.concatenate([head, tail], axis=1).astype(BF16)

    cp_t.wait()
    partial = jnp.zeros((q_dev, virt), F32)
    for t in range(chunks):
        others = x_all.at[t, pl.ds(0, (rows_n - 1) * tall), :]
        pltpu.make_async_copy(others, others, xr.at[t]).wait()
        for kb in range(BLOCKS):
            start = (t * BLOCKS + kb) * WIDTH
            width = min(WIDTH, depth - start)
            if width <= 0:
                continue
            q = iota((q_dev, LANES), 0)
            source = lax.div(q, q_own) * tall + kb * q_own + lax.rem(q, q_own)
            pick = jnp.where(source == iota((q_dev, LANES), 1), 1.0, 0.0).astype(BF16)
            g = jnp.dot(pick, x_all[t], preferred_element_type=F32).astype(BF16)
            partial = partial + lax.dot_general(
                g[:, :width], t_buf[:, pl.ds(start, width)], NT, preferred_element_type=F32
            )

    cp_w.wait()
    half = jnp.dot(split(partial), w_buf[...], preferred_element_type=F32)
    half = split(half[:q_dev] + half[q_dev:])

    def partial_copy(aux, source, to):
        return pltpu.make_async_remote_copy(
            src_ref=d_buf.at[to],
            dst_ref=r_buf.at[aux, source],
            send_sem=ds.at[0],
            recv_sem=dr.at[aux],
            device_id={"col": to, "aux": hub},
            device_id_type=MESH,
        )

    quads = cols_n // QUAD
    my_quad = lax.div(me_c, QUAD)
    lower = lax.rem(iota((q_dev // 2, LANES), 1), 2 * TAIL) < TAIL
    for step in range(quads):
        quad = lax.rem(my_quad + (2, 1, 3, 0)[step], quads)
        lanes = QUAD // 2 * pair
        part = spread[:, pl.ds(pl.multiple_of(quad * lanes, lanes), lanes)]
        slots = jnp.dot(half, part, preferred_element_type=F32)
        slots = slots[:q_dev] + slots[q_dev:]
        for j in range(QUAD):
            to = quad * QUAD + j
            first = j // 2 * pair
            head = slots[:, first + j % 2 * LANES : first + (j % 2 + 1) * LANES]
            tail = slots[:, first + 2 * LANES : first + 3 * LANES]
            upper_q, lower_q = tail[: q_dev // 2], tail[q_dev // 2 :]
            if j % 2:
                upper_q = pltpu.roll(upper_q, LANES - TAIL, 1)
            else:
                lower_q = pltpu.roll(lower_q, TAIL, 1)
            d_buf[to, pl.ds(0, q_dev), :] = head
            d_buf[to, pl.ds(q_dev, q_dev // 2), :] = jnp.where(lower, upper_q, lower_q)
        for k in (2, 1, 3, 0):
            to = quad * QUAD + lax.rem(me_c + k, QUAD)
            if step < quads - 1 or k:
                partial_copy(me_a, me_c, to).start()
            else:

                @pl.when(jnp.logical_not(summing))
                def _():
                    partial_copy(me_a, me_c, to).start()

    for t in range(chunks):
        sent = x_all.at[t, pl.ds(0, (rows_n - 1) * tall), :]
        pltpu.make_async_copy(sent, sent, xs.at[t]).wait()
    def slot_copy(aux, source, to):
        return pltpu.make_async_remote_copy(
            src_ref=z_buf.at[aux, pl.ds(pl.multiple_of(to * HEAD, HEAD), HEAD), :],
            dst_ref=z_all.at[pl.ds(pl.multiple_of(source * HEAD, HEAD), HEAD), :],
            send_sem=zs.at[aux],
            recv_sem=zr.at[0],
            device_id={"row": to, "aux": aux},
            device_id_type=MESH,
        )

    @pl.when(summing)
    def _():
        for aux in (hub,) + tuple(range(hub)):
            if aux == hub:
                others = r_buf.at[aux, pl.ds(0, cols_n - 1)]
                total = d_buf[me_c]
            else:
                others = r_buf.at[aux]
                total = jnp.zeros((dense, LANES), F32)
            pltpu.make_async_copy(others, others, dr.at[aux]).wait()
            for k in range(1 if aux == hub else 0, cols_n):
                total = total + r_buf[aux, lax.rem(me_c + k, cols_n)]
            total = jnp.concatenate([total, jnp.zeros((LANES - dense, LANES), F32)], axis=0)
            z_buf[aux] = total.T.astype(BF16)
            for k in order:
                slot_copy(aux, me_r, row_at(k)).start()
            if aux != hub:
                slot_copy(aux, me_r, me_r).start()
        own = pl.ds(pl.multiple_of(me_r * HEAD, HEAD), HEAD)
        z_all[own, :] = z_buf[hub, own, :]
        partials_sent = d_buf.at[pl.ds(0, cols_n - 1)]
        pltpu.make_async_copy(partials_sent, partials_sent, ds.at[0]).wait()
        others = z_all.at[pl.ds(0, (rows_n - 1) * HEAD), :]
        pltpu.make_async_copy(others, others, zr.at[0]).wait()

    @pl.when(jnp.logical_not(summing))
    def _():
        pltpu.make_async_copy(d_buf, d_buf, ds.at[0]).wait()
        pltpu.make_async_copy(z_all, z_all, zr.at[0]).wait()

    got = jnp.concatenate([z_all[pl.ds(i * HEAD, HEAD), :] for i in range(rows_n)], axis=1)
    result = jnp.dot(got, expand[...], preferred_element_type=F32)
    wide = rows_n * q_dev
    tail = jnp.concatenate(
        [result[:TAIL, wide : wide + LANES], result[TAIL:, wide + LANES :]], axis=1
    )
    out[...] = jnp.concatenate([result[:, :wide], tail], axis=0).astype(BF16)

    @pl.when(summing)
    def _():
        for aux in range(aux_n):
            parts = rows_n - 1 if aux == hub else rows_n
            slots_sent = z_buf.at[aux, pl.ds(0, parts * HEAD), :]
            pltpu.make_async_copy(slots_sent, slots_sent, zs.at[aux]).wait()


def shards(panels, amplitudes, virt_coeff, row_owner):
    rows_n = lax.axis_size("row")
    cols_n = lax.axis_size("col")
    aux_n = lax.axis_size("aux")
    q_own, depth = panels.shape
    nao, virt = virt_coeff.shape
    q_dev = rows_n * q_own
    chunks = -(-depth // (BLOCKS * WIDTH))
    tall = BLOCKS * q_own
    padded = -(-nao // WIDTH) * WIDTH
    dense = q_dev + q_dev // 2
    vmem = pltpu.VMEM
    dma = pltpu.SemaphoreType.DMA
    return pl.pallas_call(
        functools.partial(kernel, rows_n, cols_n, aux_n),
        out_shape=pltpu.VMEM((HEAD + TAIL, rows_n * q_dev), BF16),
        in_specs=[pl.BlockSpec(memory_space=pl.ANY)] * 4,
        out_specs=pl.BlockSpec(memory_space=pltpu.VMEM),
        scratch_shapes=[
            vmem(amplitudes.shape, BF16),
            vmem((virt, nao), BF16),
            vmem(panels.shape, BF16),
            vmem((1, nao), jnp.int32),
            vmem((1, padded), jnp.int32),
            vmem((chunks, tall, WIDTH), F32),
            vmem((chunks, rows_n * tall, WIDTH), BF16),
            vmem((padded, LANES), F32),
            vmem((nao, cols_n // 2 * 3 * LANES), BF16),
            vmem((rows_n * LANES, 2 * rows_n * q_dev), BF16),
            vmem((cols_n, dense, LANES), F32),
            vmem((aux_n, cols_n, dense, LANES), F32),
            vmem((aux_n, rows_n * HEAD, LANES), BF16),
            vmem((rows_n * HEAD, LANES), BF16),
            dma((4,)),
            dma((chunks,)),
            dma((chunks,)),
            dma((1,)),
            dma((aux_n,)),
            dma((aux_n,)),
            dma((1,)),
        ],
        compiler_params=pltpu.CompilerParams(
            collective_id=0, has_side_effects=True, vmem_limit_bytes=56 * 1024 * 1024
        ),
        cost_estimate=pl.CostEstimate(
            flops=2 * virt * depth * LANES, bytes_accessed=amplitudes.size * 2, transcendentals=0
        ),
        name="density",
    )(panels, row_owner.reshape(1, nao), amplitudes, virt_coeff.T)


def solution(mesh):
    placed = (P(("aux", "row"), "col"), P("row", "col"), P(), P())
    return jax.shard_map(
        shards, mesh=mesh, in_specs=placed, out_specs=P(("row", "col"), "aux"), check_vma=False
    )
```

```python
import functools
import jax
import jax.numpy as jnp
from jax import lax
from jax.experimental import pallas as pl
from jax.experimental.pallas import tpu as pltpu
from jax.sharding import PartitionSpec as P

F32 = jnp.float32
BF16 = jnp.bfloat16
MESH = pl.DeviceIdType.MESH
NT = (((1,), (1,)), ((), ()))

LANES = 128
BLOCKS = 4
WIDTH = 256
HEAD = 16
TAIL = 8
QUAD = 4


def split(x):
    hi = x.astype(BF16)
    lo = (x - hi.astype(F32)).astype(BF16)
    return jnp.concatenate([hi, lo], axis=0)


def iota(shape, dim):
    return lax.broadcasted_iota(jnp.int32, shape, dim)


def kernel(
    rows_n,
    cols_n,
    aux_n,
    panels,
    owner,
    amp,
    coeff_t,
    out,
    t_buf,
    w_buf,
    p_buf,
    o_buf,
    names,
    x_stage,
    x_all,
    place,
    spread,
    expand,
    d_buf,
    r_buf,
    z_buf,
    z_all,
    local_sem,
    xs,
    xr,
    ds,
    dr,
    zs,
    zr,
):
    me_r = lax.axis_index("row")
    me_c = lax.axis_index("col")
    me_a = lax.axis_index("aux")
    hub = aux_n - 1
    summing = me_a == hub
    q_own, depth = panels.shape
    virt, nao = coeff_t.shape
    q_dev = rows_n * q_own
    chunks = x_all.shape[0]
    tall = BLOCKS * q_own
    count = rows_n * cols_n
    dense = q_dev + q_dev // 2
    pair = 3 * LANES
    order = (4, 3, 5, 2, 6, 1, 7)
    far = (10, 6, 9, 11, 5, 7, 8, 2, 14, 13, 15, 12, 4, 3, 1)

    def row_at(k):
        return lax.rem(me_r + k, rows_n)

    barrier = pltpu.get_barrier_semaphore()
    def greet(**to):
        pl.semaphore_signal(barrier, inc=1, device_id=to, device_id_type=MESH)

    for k in order:
        greet(row=row_at(k))
    @pl.when(summing)
    def _():
        for k in far + (0,):
            greet(col=lax.rem(me_c + k, cols_n), aux=0)
        for k in far:
            greet(col=lax.rem(me_c + k, cols_n))

    @pl.when(jnp.logical_not(summing))
    def _():
        for k in order + (0,):
            greet(row=row_at(k), aux=hub)

    cp_p = pltpu.make_async_copy(panels, p_buf, local_sem.at[0])
    cp_o = pltpu.make_async_copy(owner, o_buf, local_sem.at[1])
    cp_t = pltpu.make_async_copy(amp, t_buf, local_sem.at[2])
    cp_w = pltpu.make_async_copy(coeff_t, w_buf, local_sem.at[3])
    cp_p.start()
    cp_o.start()
    cp_t.start()
    cp_w.start()

    x_stage[...] = jnp.zeros_like(x_stage)
    cp_p.wait()
    for t in range(chunks):
        for kb in range(BLOCKS):
            start = (t * BLOCKS + kb) * WIDTH
            width = min(WIDTH, depth - start)
            if width > 0:
                x_stage[t, pl.ds(kb * q_own, q_own), pl.ds(0, width)] = p_buf[
                    :, pl.ds(start, width)
                ].astype(F32)
    own_rows = pl.ds(pl.multiple_of(me_r * tall, tall), tall)
    for t in range(chunks):
        x_all[t, own_rows, :] = x_stage[t].astype(BF16)

    @pl.when(summing)
    def _():
        pl.semaphore_wait(barrier, 2 * rows_n - 1 + cols_n - 1)

    @pl.when(jnp.logical_not(summing))
    def _():
        pl.semaphore_wait(barrier, rows_n - 1 + cols_n)


    def panel_copy(t, source, to):
        rows = x_all.at[t, pl.ds(pl.multiple_of(source * tall, tall), tall), :]
        return pltpu.make_async_remote_copy(
            src_ref=rows,
            dst_ref=rows,
            send_sem=xs.at[t],
            recv_sem=xr.at[t],
            device_id={"row": to},
            device_id_type=MESH,
        )

    for t in range(chunks):
        for k in order:
            panel_copy(t, me_r, row_at(k)).start()

    names[...] = jnp.full_like(names, -1)
    cp_o.wait()
    names[:, pl.ds(0, nao)] = o_buf[...]
    tri = (iota((WIDTH, WIDTH), 0) < iota((WIDTH, WIDTH), 1)).astype(BF16)
    carry = jnp.zeros((count, 1), F32)
    for b in range(names.shape[1] // WIDTH):
        name = names[:, pl.ds(b * WIDTH, WIDTH)]
        ones = jnp.where(name == iota((count, WIDTH), 0), 1.0, 0.0).astype(F32)
        before = jnp.dot(ones.astype(BF16), tri, preferred_element_type=F32) + carry
        slot = jnp.sum(ones * before, axis=0, keepdims=True)
        carry = carry + jnp.sum(ones, axis=1, keepdims=True)
        at_row = lax.div(name, jnp.int32(cols_n))
        at_col = name - at_row * cols_n
        at_pair = lax.div(at_col, jnp.int32(2))
        odd = at_col - at_pair * 2
        base = (at_pair * pair + at_row * HEAD).astype(F32)
        early = base + (odd * LANES).astype(F32) + slot
        late = base + (odd * TAIL + (2 * LANES - HEAD)).astype(F32) + slot
        lane = jnp.where(slot < HEAD, early, late)
        lane = jnp.where(name < 0, -1.0, lane)
        place[pl.ds(b * WIDTH, WIDTH), :] = jnp.broadcast_to(lane, (LANES, WIDTH)).T

    @pl.loop(0, spread.shape[1] // LANES)
    def _(b):
        at = (iota((nao, LANES), 1) + b * LANES).astype(F32)
        hot = jnp.where(place[pl.ds(0, nao), :] == at, 1.0, 0.0)
        spread[:, pl.ds(pl.multiple_of(b * LANES, LANES), LANES)] = hot.astype(BF16)

    for i in range(rows_n):
        a = iota((LANES, rows_n * q_dev), 0)
        n = iota((LANES, rows_n * q_dev), 1)
        head = jnp.where((a < q_dev) & (n == a * rows_n + i), 1.0, 0.0)
        tail = jnp.where(
            (a >= q_dev) & (a < dense) & (lax.rem(n, LANES) == (a - q_dev) * rows_n + i), 1.0, 0.0
        )
        expand[pl.ds(i * LANES, LANES), :] = jnp.concatenate([head, tail], axis=1).astype(BF16)

    cp_t.wait()
    partial = jnp.zeros((q_dev, virt), F32)
    for t in range(chunks):
        others = x_all.at[t, pl.ds(0, (rows_n - 1) * tall), :]
        pltpu.make_async_copy(others, others, xr.at[t]).wait()
        for kb in range(BLOCKS):
            start = (t * BLOCKS + kb) * WIDTH
            width = min(WIDTH, depth - start)
            if width <= 0:
                continue
            q = iota((q_dev, LANES), 0)
            source = lax.div(q, q_own) * tall + kb * q_own + lax.rem(q, q_own)
            pick = jnp.where(source == iota((q_dev, LANES), 1), 1.0, 0.0).astype(BF16)
            g = jnp.dot(pick, x_all[t], preferred_element_type=F32).astype(BF16)
            partial = partial + lax.dot_general(
                g[:, :width], t_buf[:, pl.ds(start, width)], NT, preferred_element_type=F32
            )

    cp_w.wait()
    half = jnp.dot(split(partial), w_buf[...], preferred_element_type=F32)
    half = split(half[:q_dev] + half[q_dev:])

    def partial_copy(aux, source, to):
        return pltpu.make_async_remote_copy(
            src_ref=d_buf.at[to],
            dst_ref=r_buf.at[aux, source],
            send_sem=ds.at[0],
            recv_sem=dr.at[aux],
            device_id={"col": to, "aux": hub},
            device_id_type=MESH,
        )

    quads = cols_n // QUAD
    my_quad = lax.div(me_c, QUAD)
    lower = lax.rem(iota((q_dev // 2, LANES), 1), 2 * TAIL) < TAIL
    for step in range(quads):
        quad = lax.rem(my_quad + (2, 1, 3, 0)[step], quads)
        lanes = QUAD // 2 * pair
        part = spread[:, pl.ds(pl.multiple_of(quad * lanes, lanes), lanes)]
        slots = jnp.dot(half, part, preferred_element_type=F32)
        slots = slots[:q_dev] + slots[q_dev:]
        for j in range(QUAD):
            to = quad * QUAD + j
            first = j // 2 * pair
            head = slots[:, first + j % 2 * LANES : first + (j % 2 + 1) * LANES]
            tail = slots[:, first + 2 * LANES : first + 3 * LANES]
            upper_q, lower_q = tail[: q_dev // 2], tail[q_dev // 2 :]
            if j % 2:
                upper_q = pltpu.roll(upper_q, LANES - TAIL, 1)
            else:
                lower_q = pltpu.roll(lower_q, TAIL, 1)
            d_buf[to, pl.ds(0, q_dev), :] = head
            d_buf[to, pl.ds(q_dev, q_dev // 2), :] = jnp.where(lower, upper_q, lower_q)
        for k in (2, 1, 3, 0):
            to = quad * QUAD + lax.rem(me_c + k, QUAD)
            if step < quads - 1 or k:
                partial_copy(me_a, me_c, to).start()
            else:

                @pl.when(jnp.logical_not(summing))
                def _():
                    partial_copy(me_a, me_c, to).start()

    for t in range(chunks):
        sent = x_all.at[t, pl.ds(0, (rows_n - 1) * tall), :]
        pltpu.make_async_copy(sent, sent, xs.at[t]).wait()
    def slot_copy(aux, source, to):
        return pltpu.make_async_remote_copy(
            src_ref=z_buf.at[aux, pl.ds(pl.multiple_of(to * HEAD, HEAD), HEAD), :],
            dst_ref=z_all.at[pl.ds(pl.multiple_of(source * HEAD, HEAD), HEAD), :],
            send_sem=zs.at[aux],
            recv_sem=zr.at[0],
            device_id={"row": to, "aux": aux},
            device_id_type=MESH,
        )

    @pl.when(summing)
    def _():
        for aux in (hub,) + tuple(range(hub)):
            if aux == hub:
                others = r_buf.at[aux, pl.ds(0, cols_n - 1)]
                total = d_buf[me_c]
            else:
                others = r_buf.at[aux]
                total = jnp.zeros((dense, LANES), F32)
            pltpu.make_async_copy(others, others, dr.at[aux]).wait()
            for k in range(1 if aux == hub else 0, cols_n):
                total = total + r_buf[aux, lax.rem(me_c + k, cols_n)]
            total = jnp.concatenate([total, jnp.zeros((LANES - dense, LANES), F32)], axis=0)
            z_buf[aux] = total.T.astype(BF16)
            for k in order:
                slot_copy(aux, me_r, row_at(k)).start()
            if aux != hub:
                slot_copy(aux, me_r, me_r).start()
        own = pl.ds(pl.multiple_of(me_r * HEAD, HEAD), HEAD)
        z_all[own, :] = z_buf[hub, own, :]
        partials_sent = d_buf.at[pl.ds(0, cols_n - 1)]
        pltpu.make_async_copy(partials_sent, partials_sent, ds.at[0]).wait()
        others = z_all.at[pl.ds(0, (rows_n - 1) * HEAD), :]
        pltpu.make_async_copy(others, others, zr.at[0]).wait()

    @pl.when(jnp.logical_not(summing))
    def _():
        pltpu.make_async_copy(d_buf, d_buf, ds.at[0]).wait()
        pltpu.make_async_copy(z_all, z_all, zr.at[0]).wait()

    got = jnp.concatenate([z_all[pl.ds(i * HEAD, HEAD), :] for i in range(rows_n)], axis=1)
    result = jnp.dot(got, expand[...], preferred_element_type=F32)
    wide = rows_n * q_dev
    tail = jnp.concatenate(
        [result[:TAIL, wide : wide + LANES], result[TAIL:, wide + LANES :]], axis=1
    )
    out[...] = jnp.concatenate([result[:, :wide], tail], axis=0).astype(BF16)

    @pl.when(summing)
    def _():
        for aux in range(aux_n):
            parts = rows_n - 1 if aux == hub else rows_n
            slots_sent = z_buf.at[aux, pl.ds(0, parts * HEAD), :]
            pltpu.make_async_copy(slots_sent, slots_sent, zs.at[aux]).wait()


def shards(panels, amplitudes, virt_coeff, row_owner):
    rows_n = lax.axis_size("row")
    cols_n = lax.axis_size("col")
    aux_n = lax.axis_size("aux")
    q_own, depth = panels.shape
    nao, virt = virt_coeff.shape
    q_dev = rows_n * q_own
    chunks = -(-depth // (BLOCKS * WIDTH))
    tall = BLOCKS * q_own
    padded = -(-nao // WIDTH) * WIDTH
    dense = q_dev + q_dev // 2
    vmem = pltpu.VMEM
    dma = pltpu.SemaphoreType.DMA
    return pl.pallas_call(
        functools.partial(kernel, rows_n, cols_n, aux_n),
        out_shape=pltpu.VMEM((HEAD + TAIL, rows_n * q_dev), BF16),
        in_specs=[pl.BlockSpec(memory_space=pl.ANY)] * 4,
        out_specs=pl.BlockSpec(memory_space=pltpu.VMEM),
        scratch_shapes=[
            vmem(amplitudes.shape, BF16),
            vmem((virt, nao), BF16),
            vmem(panels.shape, BF16),
            vmem((1, nao), jnp.int32),
            vmem((1, padded), jnp.int32),
            vmem((chunks, tall, WIDTH), F32),
            vmem((chunks, rows_n * tall, WIDTH), BF16),
            vmem((padded, LANES), F32),
            vmem((nao, cols_n // 2 * 3 * LANES), BF16),
            vmem((rows_n * LANES, 2 * rows_n * q_dev), BF16),
            vmem((cols_n, dense, LANES), F32),
            vmem((aux_n, cols_n, dense, LANES), F32),
            vmem((aux_n, rows_n * HEAD, LANES), BF16),
            vmem((rows_n * HEAD, LANES), BF16),
            dma((4,)),
            dma((chunks,)),
            dma((chunks,)),
            dma((1,)),
            dma((aux_n,)),
            dma((aux_n,)),
            dma((1,)),
        ],
        compiler_params=pltpu.CompilerParams(
            collective_id=0, has_side_effects=True, vmem_limit_bytes=56 * 1024 * 1024
        ),
        cost_estimate=pl.CostEstimate(
            flops=2 * virt * depth * LANES, bytes_accessed=amplitudes.size * 2, transcendentals=0
        ),
        name="density",
    )(panels, row_owner.reshape(1, nao), amplitudes, virt_coeff.T)


def solution(mesh):
    placed = (P(("aux", "row"), "col"), P("row", "col"), P(), P())
    return jax.shard_map(
        shards, mesh=mesh, in_specs=placed, out_specs=P(("row", "col"), "aux"), check_vma=False
    )
```

```python
import functools
import jax
import jax.numpy as jnp
from jax import lax
from jax.experimental import pallas as pl
from jax.experimental.pallas import tpu as pltpu
from jax.sharding import PartitionSpec as P

F32 = jnp.float32
BF16 = jnp.bfloat16
MESH = pl.DeviceIdType.MESH
NT = (((1,), (1,)), ((), ()))

LANES = 128
BLOCKS = 4
WIDTH = 256
HEAD = 16
TAIL = 8
QUAD = 4


def split(x):
    hi = x.astype(BF16)
    lo = (x - hi.astype(F32)).astype(BF16)
    return jnp.concatenate([hi, lo], axis=0)


def iota(shape, dim):
    return lax.broadcasted_iota(jnp.int32, shape, dim)


def kernel(
    rows_n,
    cols_n,
    aux_n,
    panels,
    owner,
    amp,
    coeff_t,
    out,
    t_buf,
    w_buf,
    p_buf,
    o_buf,
    names,
    x_stage,
    x_all,
    place,
    spread,
    expand,
    d_buf,
    r_buf,
    z_buf,
    z_all,
    local_sem,
    xs,
    xr,
    ds,
    dr,
    zs,
    zr,
):
    me_r = lax.axis_index("row")
    me_c = lax.axis_index("col")
    me_a = lax.axis_index("aux")
    hub = aux_n - 1
    summing = me_a == hub
    q_own, depth = panels.shape
    virt, nao = coeff_t.shape
    q_dev = rows_n * q_own
    chunks = x_all.shape[0]
    tall = BLOCKS * q_own
    count = rows_n * cols_n
    dense = q_dev + q_dev // 2
    pair = 3 * LANES
    order = (4, 3, 5, 2, 6, 1, 7)
    far = (10, 6, 9, 11, 5, 7, 8, 2, 14, 13, 15, 12, 4, 3, 1)

    def row_at(k):
        return lax.rem(me_r + k, rows_n)

    barrier = pltpu.get_barrier_semaphore()
    def greet(**to):
        pl.semaphore_signal(barrier, inc=1, device_id=to, device_id_type=MESH)

    for k in order:
        greet(row=row_at(k))
    @pl.when(summing)
    def _():
        for k in far + (0,):
            greet(col=lax.rem(me_c + k, cols_n), aux=0)
        for k in far:
            greet(col=lax.rem(me_c + k, cols_n))

    @pl.when(jnp.logical_not(summing))
    def _():
        for k in order + (0,):
            greet(row=row_at(k), aux=hub)

    cp_p = pltpu.make_async_copy(panels, p_buf, local_sem.at[0])
    cp_o = pltpu.make_async_copy(owner, o_buf, local_sem.at[1])
    cp_t = pltpu.make_async_copy(amp, t_buf, local_sem.at[2])
    cp_w = pltpu.make_async_copy(coeff_t, w_buf, local_sem.at[3])
    cp_p.start()
    cp_o.start()
    cp_t.start()
    cp_w.start()

    def fill_slots():
        names[...] = jnp.full_like(names, -1)
        cp_o.wait()
        names[:, pl.ds(0, nao)] = o_buf[...]
        tri = (iota((WIDTH, WIDTH), 0) < iota((WIDTH, WIDTH), 1)).astype(BF16)
        carry = jnp.zeros((count, 1), F32)
        for b in range(names.shape[1] // WIDTH):
            name = names[:, pl.ds(b * WIDTH, WIDTH)]
            ones = jnp.where(name == iota((count, WIDTH), 0), 1.0, 0.0).astype(F32)
            before = jnp.dot(ones.astype(BF16), tri, preferred_element_type=F32) + carry
            slot = jnp.sum(ones * before, axis=0, keepdims=True)
            carry = carry + jnp.sum(ones, axis=1, keepdims=True)
            at_row = lax.div(name, jnp.int32(cols_n))
            at_col = name - at_row * cols_n
            at_pair = lax.div(at_col, jnp.int32(2))
            odd = at_col - at_pair * 2
            base = (at_pair * pair + at_row * HEAD).astype(F32)
            early = base + (odd * LANES).astype(F32) + slot
            late = base + (odd * TAIL + (2 * LANES - HEAD)).astype(F32) + slot
            lane = jnp.where(slot < HEAD, early, late)
            lane = jnp.where(name < 0, -1.0, lane)
            place[pl.ds(b * WIDTH, WIDTH), :] = jnp.broadcast_to(lane, (LANES, WIDTH)).T

        @pl.loop(0, spread.shape[1] // LANES)
        def _(b):
            at = (iota((nao, LANES), 1) + b * LANES).astype(F32)
            hot = jnp.where(place[pl.ds(0, nao), :] == at, 1.0, 0.0)
            spread[:, pl.ds(pl.multiple_of(b * LANES, LANES), LANES)] = hot.astype(BF16)

    x_stage[...] = jnp.zeros_like(x_stage)
    cp_p.wait()
    for t in range(chunks):
        for kb in range(BLOCKS):
            start = (t * BLOCKS + kb) * WIDTH
            width = min(WIDTH, depth - start)
            if width > 0:
                x_stage[t, pl.ds(kb * q_own, q_own), pl.ds(0, width)] = p_buf[
                    :, pl.ds(start, width)
                ].astype(F32)
    own_rows = pl.ds(pl.multiple_of(me_r * tall, tall), tall)
    for t in range(chunks):
        x_all[t, own_rows, :] = x_stage[t].astype(BF16)

    early = me_r < rows_n // 2

    @pl.when(early)
    def _():
        fill_slots()

    @pl.when(summing)
    def _():
        pl.semaphore_wait(barrier, 2 * rows_n - 1 + cols_n - 1)

    @pl.when(jnp.logical_not(summing))
    def _():
        pl.semaphore_wait(barrier, rows_n - 1 + cols_n)


    def panel_copy(t, source, to):
        rows = x_all.at[t, pl.ds(pl.multiple_of(source * tall, tall), tall), :]
        return pltpu.make_async_remote_copy(
            src_ref=rows,
            dst_ref=rows,
            send_sem=xs.at[t],
            recv_sem=xr.at[t],
            device_id={"row": to},
            device_id_type=MESH,
        )

    for t in range(chunks):
        for k in order:
            panel_copy(t, me_r, row_at(k)).start()

    @pl.when(jnp.logical_not(early))
    def _():
        fill_slots()

    for i in range(rows_n):
        a = iota((LANES, rows_n * q_dev), 0)
        n = iota((LANES, rows_n * q_dev), 1)
        head = jnp.where((a < q_dev) & (n == a * rows_n + i), 1.0, 0.0)
        tail = jnp.where(
            (a >= q_dev) & (a < dense) & (lax.rem(n, LANES) == (a - q_dev) * rows_n + i), 1.0, 0.0
        )
        expand[pl.ds(i * LANES, LANES), :] = jnp.concatenate([head, tail], axis=1).astype(BF16)

    cp_t.wait()
    partial = jnp.zeros((q_dev, virt), F32)
    for t in range(chunks):
        others = x_all.at[t, pl.ds(0, (rows_n - 1) * tall), :]
        pltpu.make_async_copy(others, others, xr.at[t]).wait()
        for kb in range(BLOCKS):
            start = (t * BLOCKS + kb) * WIDTH
            width = min(WIDTH, depth - start)
            if width <= 0:
                continue
            q = iota((q_dev, LANES), 0)
            source = lax.div(q, q_own) * tall + kb * q_own + lax.rem(q, q_own)
            pick = jnp.where(source == iota((q_dev, LANES), 1), 1.0, 0.0).astype(BF16)
            g = jnp.dot(pick, x_all[t], preferred_element_type=F32).astype(BF16)
            partial = partial + lax.dot_general(
                g[:, :width], t_buf[:, pl.ds(start, width)], NT, preferred_element_type=F32
            )

    cp_w.wait()
    half = jnp.dot(split(partial), w_buf[...], preferred_element_type=F32)
    half = split(half[:q_dev] + half[q_dev:])

    def partial_copy(aux, source, to):
        return pltpu.make_async_remote_copy(
            src_ref=d_buf.at[to],
            dst_ref=r_buf.at[aux, source],
            send_sem=ds.at[0],
            recv_sem=dr.at[aux],
            device_id={"col": to, "aux": hub},
            device_id_type=MESH,
        )

    quads = cols_n // QUAD
    my_quad = lax.div(me_c, QUAD)
    lower = lax.rem(iota((q_dev // 2, LANES), 1), 2 * TAIL) < TAIL
    for step in range(quads):
        quad = lax.rem(my_quad + (2, 1, 3, 0)[step], quads)
        lanes = QUAD // 2 * pair
        part = spread[:, pl.ds(pl.multiple_of(quad * lanes, lanes), lanes)]
        slots = jnp.dot(half, part, preferred_element_type=F32)
        slots = slots[:q_dev] + slots[q_dev:]
        for j in range(QUAD):
            to = quad * QUAD + j
            first = j // 2 * pair
            head = slots[:, first + j % 2 * LANES : first + (j % 2 + 1) * LANES]
            tail = slots[:, first + 2 * LANES : first + 3 * LANES]
            upper_q, lower_q = tail[: q_dev // 2], tail[q_dev // 2 :]
            if j % 2:
                upper_q = pltpu.roll(upper_q, LANES - TAIL, 1)
            else:
                lower_q = pltpu.roll(lower_q, TAIL, 1)
            d_buf[to, pl.ds(0, q_dev), :] = head
            d_buf[to, pl.ds(q_dev, q_dev // 2), :] = jnp.where(lower, upper_q, lower_q)
        for k in (2, 1, 3, 0):
            to = quad * QUAD + lax.rem(me_c + k, QUAD)
            if step < quads - 1 or k:
                partial_copy(me_a, me_c, to).start()
            else:

                @pl.when(jnp.logical_not(summing))
                def _():
                    partial_copy(me_a, me_c, to).start()

    for t in range(chunks):
        sent = x_all.at[t, pl.ds(0, (rows_n - 1) * tall), :]
        pltpu.make_async_copy(sent, sent, xs.at[t]).wait()
    def slot_copy(aux, source, to):
        return pltpu.make_async_remote_copy(
            src_ref=z_buf.at[aux, pl.ds(pl.multiple_of(to * HEAD, HEAD), HEAD), :],
            dst_ref=z_all.at[pl.ds(pl.multiple_of(source * HEAD, HEAD), HEAD), :],
            send_sem=zs.at[aux],
            recv_sem=zr.at[0],
            device_id={"row": to, "aux": aux},
            device_id_type=MESH,
        )

    @pl.when(summing)
    def _():
        for aux in (hub,) + tuple(range(hub)):
            if aux == hub:
                others = r_buf.at[aux, pl.ds(0, cols_n - 1)]
                total = d_buf[me_c]
            else:
                others = r_buf.at[aux]
                total = jnp.zeros((dense, LANES), F32)
            pltpu.make_async_copy(others, others, dr.at[aux]).wait()
            for k in range(1 if aux == hub else 0, cols_n):
                total = total + r_buf[aux, lax.rem(me_c + k, cols_n)]
            total = jnp.concatenate([total, jnp.zeros((LANES - dense, LANES), F32)], axis=0)
            z_buf[aux] = total.T.astype(BF16)
            for k in order:
                slot_copy(aux, me_r, row_at(k)).start()
            if aux != hub:
                slot_copy(aux, me_r, me_r).start()
        own = pl.ds(pl.multiple_of(me_r * HEAD, HEAD), HEAD)
        z_all[own, :] = z_buf[hub, own, :]
        partials_sent = d_buf.at[pl.ds(0, cols_n - 1)]
        pltpu.make_async_copy(partials_sent, partials_sent, ds.at[0]).wait()
        others = z_all.at[pl.ds(0, (rows_n - 1) * HEAD), :]
        pltpu.make_async_copy(others, others, zr.at[0]).wait()

    @pl.when(jnp.logical_not(summing))
    def _():
        pltpu.make_async_copy(d_buf, d_buf, ds.at[0]).wait()
        pltpu.make_async_copy(z_all, z_all, zr.at[0]).wait()

    got = jnp.concatenate([z_all[pl.ds(i * HEAD, HEAD), :] for i in range(rows_n)], axis=1)
    result = jnp.dot(got, expand[...], preferred_element_type=F32)
    wide = rows_n * q_dev
    tail = jnp.concatenate(
        [result[:TAIL, wide : wide + LANES], result[TAIL:, wide + LANES :]], axis=1
    )
    out[...] = jnp.concatenate([result[:, :wide], tail], axis=0).astype(BF16)

    @pl.when(summing)
    def _():
        for aux in range(aux_n):
            parts = rows_n - 1 if aux == hub else rows_n
            slots_sent = z_buf.at[aux, pl.ds(0, parts * HEAD), :]
            pltpu.make_async_copy(slots_sent, slots_sent, zs.at[aux]).wait()


def shards(panels, amplitudes, virt_coeff, row_owner):
    rows_n = lax.axis_size("row")
    cols_n = lax.axis_size("col")
    aux_n = lax.axis_size("aux")
    q_own, depth = panels.shape
    nao, virt = virt_coeff.shape
    q_dev = rows_n * q_own
    chunks = -(-depth // (BLOCKS * WIDTH))
    tall = BLOCKS * q_own
    padded = -(-nao // WIDTH) * WIDTH
    dense = q_dev + q_dev // 2
    vmem = pltpu.VMEM
    dma = pltpu.SemaphoreType.DMA
    return pl.pallas_call(
        functools.partial(kernel, rows_n, cols_n, aux_n),
        out_shape=pltpu.VMEM((HEAD + TAIL, rows_n * q_dev), BF16),
        in_specs=[pl.BlockSpec(memory_space=pl.ANY)] * 4,
        out_specs=pl.BlockSpec(memory_space=pltpu.VMEM),
        scratch_shapes=[
            vmem(amplitudes.shape, BF16),
            vmem((virt, nao), BF16),
            vmem(panels.shape, BF16),
            vmem((1, nao), jnp.int32),
            vmem((1, padded), jnp.int32),
            vmem((chunks, tall, WIDTH), F32),
            vmem((chunks, rows_n * tall, WIDTH), BF16),
            vmem((padded, LANES), F32),
            vmem((nao, cols_n // 2 * 3 * LANES), BF16),
            vmem((rows_n * LANES, 2 * rows_n * q_dev), BF16),
            vmem((cols_n, dense, LANES), F32),
            vmem((aux_n, cols_n, dense, LANES), F32),
            vmem((aux_n, rows_n * HEAD, LANES), BF16),
            vmem((rows_n * HEAD, LANES), BF16),
            dma((4,)),
            dma((chunks,)),
            dma((chunks,)),
            dma((1,)),
            dma((aux_n,)),
            dma((aux_n,)),
            dma((1,)),
        ],
        compiler_params=pltpu.CompilerParams(
            collective_id=0, has_side_effects=True, vmem_limit_bytes=56 * 1024 * 1024
        ),
        cost_estimate=pl.CostEstimate(
            flops=2 * virt * depth * LANES, bytes_accessed=amplitudes.size * 2, transcendentals=0
        ),
        name="density",
    )(panels, row_owner.reshape(1, nao), amplitudes, virt_coeff.T)


def solution(mesh):
    placed = (P(("aux", "row"), "col"), P("row", "col"), P(), P())
    return jax.shard_map(
        shards, mesh=mesh, in_specs=placed, out_specs=P(("row", "col"), "aux"), check_vma=False
    )
```
